512 devices in a mesh: dp: 32 (over y, x, core), ctx: 16 (over z).
Axes of the slice: x: 4, y: 4, z: 16, core: 2. Of those that a mesh axis runs over, the one named last changes fastest.
Arguments:
- queries: bfloat16 [65536, 2048], P(('dp', 'ctx')), parts along dimension 0, may hold values from -6 to 6
- keys: bfloat16 [65536, 512], P(('dp', 'ctx')), parts along dimension 0, may hold values from -6 to 6
- values: bfloat16 [65536, 512], P(('dp', 'ctx')), parts along dimension 0, may hold values from -6 to 6
- out_grad: bfloat16 [65536, 2048], P(('dp', 'ctx')), parts along dimension 0, may hold values from -6 to 6
- segment_ids: int32 [65536], P('dp'), parts along dimension 0, may hold values from 0 to 5, never falling along the last dimension, each value on 1 to 1536 neighbouring positions
Outputs:
- attended: bfloat16 [65536, 2048], P(('dp', 'ctx')), parts along dimension 0
- grad_query: bfloat16 [65536, 2048], P(('dp', 'ctx')), parts along dimension 0
- grad_key: float32 [65536, 512], P(('dp', 'ctx')), parts along dimension 0
- grad_value: float32 [65536, 512], P(('dp', 'ctx')), parts along dimension 0
The draws below stay inside these ranges and needn't reach their ends.
There are 32 independent parts, one for each index of `dp`. The reference program is written for one: setup_inputs(seed, part) draws one part's arguments, and reference() takes and returns one part's arrays. A program takes and returns all parts, laid end to end along the dimension named above; each array names one. Nothing has to cross between parts.
Inputs may be any that keep to these rules, and one draw needn't show every extreme that they name: `segment_ids`: ids never fall along the window.
All inputs are finite; a program needn't handle non-finite values.
Results may differ from the reference program's by a relative error of at most 0.025.
Values may be sent and summed in bfloat16 or wider, within the bound.
No kernel may reach another device: no remote copies, remote signals or barrier semaphores. Data moves between devices by JAX's collectives and lax.ppermute only.
A program may use at most 128 MiB of HBM per device.

```python
import math
import jax
import jax.numpy as jnp
import numpy as np
from jax import lax

H = 16
KVH = 4
HD = 128
GROUP = 4
SEGS = 6
TOKENS = 2048


def draw_queries(key, part):
    key = jax.random.fold_in(key, 1)
    base = jnp.clip(jax.random.normal(key, (TOKENS, H * HD), jnp.float32), -4.0, 4.0)
    return base.astype(jnp.bfloat16)


def draw_keys(key, part):
    key = jax.random.fold_in(key, 2)
    base = jnp.clip(jax.random.normal(key, (TOKENS, KVH * HD), jnp.float32), -4.0, 4.0)
    return base.astype(jnp.bfloat16)


def shard_levels(stream_key, dims, split, smallest, top_value):
    def one(position, parts):
        heights = jax.random.uniform(jax.random.fold_in(jax.random.fold_in(stream_key, 6), position), (parts,), jnp.float32, smallest / len(split), top_value / len(split))
        return jnp.repeat(jnp.exp(heights), dims[position] // parts).reshape((-1,) + (1,) * (len(dims) - position - 1))

    level = one(*split[0])
    for cut in split[1:]:
        level = level * one(*cut)
    return level


def profile(count, total, bound, lean):
    portions = [(1 << 20) // math.isqrt(grade ** lean) + 1 for grade in range(2, count + 1)]
    rest, holding = total - bound - (count - 1), [1] * (count - 1)
    while rest > 0:
        candidates = [i for i in range(count - 1) if holding[i] < bound]
        whole, left = sum([portions[i] for i in candidates]), rest
        for i in candidates:
            more = min(bound - holding[i], max(1, left * portions[i] // whole), rest)
            holding[i] = holding[i] + more
            rest = rest - more
    return np.array([bound] + holding)


def ragged_sizes(stream_key, amount, total, most, lean):
    if amount == 2:
        one = jax.random.randint(stream_key, (), max(1, total - most), min(most, total - 1) + 1)
        return jnp.stack([one, total - one])
    lengths = jnp.asarray(profile(amount, total, most, lean), jnp.int32)
    pairs = (amount - 1) // 2
    donor, taker = lengths[1:1 + 2 * pairs:2], lengths[2:2 + 2 * pairs:2]
    slack = jnp.minimum(donor - 1, most - taker)
    passed = jax.random.randint(jax.random.fold_in(stream_key, 1), (pairs,), 0, 1 << 20) % (slack + 1)
    lengths = lengths.at[1:1 + 2 * pairs:2].set(donor - passed).at[2:2 + 2 * pairs:2].set(taker + passed)
    return lengths[jax.random.permutation(jax.random.fold_in(stream_key, 2), amount)]


def normal_values(own_key, dims, scale, reach, cuts=(), held_as=jnp.bfloat16):
    result = scale * jax.random.normal(own_key, dims, jnp.float32)
    if cuts:
        result = result * shard_levels(own_key, dims, cuts, -0.22, 0.18)
    return jnp.clip(result, -reach, reach).astype(held_as)


def setup_inputs(seed: int = 0, part: int = 0) -> dict:
    streams_of = jax.random.split(jax.random.key(seed), 6)
    own_keys = jax.random.split(jax.random.fold_in(streams_of[5], part), 6)
    queries = draw_queries(jax.random.fold_in(jax.random.fold_in(streams_of[5], part), 71), part)
    keys = draw_keys(jax.random.fold_in(jax.random.fold_in(streams_of[5], part), 71), part)
    values = normal_values(own_keys[2], (TOKENS, KVH * HD), 1.0, 6.0, ((0, 16),))
    out_grad = normal_values(own_keys[3], (TOKENS, H * HD), 1.0, 6.0, ((0, 16),))
    segment_ids = jnp.searchsorted(jnp.cumsum(ragged_sizes(own_keys[4], SEGS, TOKENS, TOKENS * 3 // 4, 0)), jnp.arange(TOKENS), side="right").astype(jnp.int32)
    return dict(queries=queries, keys=keys, values=values, out_grad=out_grad, segment_ids=segment_ids)


neg_big = -1e+30

def reference(queries, keys, values, out_grad, segment_ids):
    all_rows = queries.shape[0]
    scale = 1.0 / math.sqrt(HD)
    q_heads = queries.reshape(all_rows, KVH, GROUP, HD).transpose(1, 2, 0, 3)
    g_heads = out_grad.reshape(all_rows, KVH, GROUP, HD).transpose(1, 2, 0, 3)
    k_heads = keys.reshape(all_rows, KVH, HD).transpose(1, 0, 2)
    v_heads = values.reshape(all_rows, KVH, HD).transpose(1, 0, 2)
    places = jnp.arange(all_rows, dtype=jnp.int32)
    allowed = (places[None, :] <= places[:, None]) & (segment_ids[None, :] == segment_ids[:, None])

    def one_group(group_in):
        q_group, g_group, k_group, v_group = group_in

        def one_head(head_in):
            q_head, g_head = head_in
            scores = jnp.dot(q_head, k_group.T, preferred_element_type=jnp.float32) * scale
            scores = jnp.where(allowed, scores, neg_big)
            top_score = lax.optimization_barrier(jnp.max(scores, axis=1))
            total = lax.optimization_barrier(jnp.sum(jnp.where(allowed, jnp.exp(scores - top_score[:, None]), 0.0), axis=1))
            log_total = top_score + jnp.log(total)
            probs = jnp.where(allowed, jnp.exp(scores - log_total[:, None]), 0.0)
            probs_low = probs.astype(jnp.bfloat16)
            attended = jnp.dot(probs_low, v_group, preferred_element_type=jnp.float32).astype(jnp.bfloat16)
            inner = lax.optimization_barrier(jnp.sum(g_head.astype(jnp.float32) * attended.astype(jnp.float32), axis=1))
            grad_probs = jnp.dot(g_head, v_group.T, preferred_element_type=jnp.float32)
            grad_scores = (probs * (grad_probs - inner[:, None]) * scale).astype(jnp.bfloat16)
            grad_query = jnp.dot(grad_scores, k_group, preferred_element_type=jnp.float32).astype(jnp.bfloat16)
            grad_key = jnp.dot(grad_scores.T, q_head, preferred_element_type=jnp.float32)
            grad_value = jnp.dot(probs_low.T, g_head, preferred_element_type=jnp.float32)
            return (attended, grad_query, grad_key, grad_value)
        outs_head = lax.map(one_head, (q_group, g_group))
        return (outs_head[0], outs_head[1], lax.optimization_barrier(jnp.sum(outs_head[2], axis=0)), lax.optimization_barrier(jnp.sum(outs_head[3], axis=0)))
    attended, grad_query, grad_key, grad_value = lax.map(one_group, (q_heads, g_heads, k_heads, v_heads))
    attended = attended.transpose(2, 0, 1, 3).reshape(all_rows, H * HD)
    grad_query = grad_query.transpose(2, 0, 1, 3).reshape(all_rows, H * HD)
    grad_key = grad_key.transpose(1, 0, 2).reshape(all_rows, KVH * HD)
    grad_value = grad_value.transpose(1, 0, 2).reshape(all_rows, KVH * HD)
    return (attended, grad_query, grad_key, grad_value)
```

```python
import math

import jax
import jax.numpy as jnp
from jax import lax
from jax.experimental import pallas as pl
from jax.experimental.pallas import tpu as pltpu
from jax.sharding import PartitionSpec as P

KVH = 4
HD = 128
GROUP = 4
CHUNK = 256

neg_big = -1e30


def dot_nt(a, b):
    return lax.dot_general(a, b, (((1,), (1,)), ((), ())), preferred_element_type=jnp.float32)


def dot_nn(a, b):
    return lax.dot_general(a, b, (((1,), (0,)), ((), ())), preferred_element_type=jnp.float32)


def dot_tn(a, b):
    return lax.dot_general(a, b, (((0,), (0,)), ((), ())), preferred_element_type=jnp.float32)


def heads_of(ref, g):
    base = g * GROUP * HD
    return jnp.concatenate(
        [ref[:, base + r * HD : base + (r + 1) * HD] for r in range(GROUP)], axis=0
    )


def attend_kernel(
    bounds, first_ref, q_ref, g_ref, kv_ref, out_ref, gq_ref, gkv_ref,
    s_ref, e_ref, acc_ref, stat_ref, low_ref,
):
    rows = q_ref.shape[0]
    stacked = rows * GROUP
    wide = KVH * HD
    scale = 1.0 / math.sqrt(HD)
    to_two = scale / math.log(2.0)
    q_start, low, high, clear_from = bounds[0], bounds[1], bounds[2], bounds[3]
    first = jnp.concatenate([first_ref[...]] * GROUP, axis=0)
    q_place = q_start + jnp.bitwise_and(
        lax.broadcasted_iota(jnp.int32, (stacked, CHUNK), 0), rows - 1
    )
    lanes = lax.broadcasted_iota(jnp.int32, (stacked, CHUNK), 1)

    gkv_ref[...] = jnp.zeros_like(gkv_ref)
    stat_ref[...] = jnp.full(stat_ref.shape, neg_big, jnp.float32)

    def scores_step(c, carry):
        at = pl.multiple_of(c * CHUNK, CHUNK)
        for g in range(KVH):
            k_block = kv_ref[pl.ds(at, CHUNK), g * HD : (g + 1) * HD]
            s_ref[g, c] = dot_nt(heads_of(q_ref, g), k_block)

        @pl.when((at < clear_from) | (at + CHUNK > q_start))
        def _():
            k_place = at + lanes
            allowed = (k_place >= first) & (k_place <= q_place)
            for g in range(KVH):
                s_ref[g, c] = jnp.where(allowed, s_ref[g, c], neg_big)

        for g in range(KVH):
            s = s_ref[g, c]
            stat_ref[g] = jnp.maximum(stat_ref[g], jnp.maximum(s[:, :HD], s[:, HD:]))
        return carry

    lax.fori_loop(low, high, scores_step, 0)

    tops = []
    for g in range(KVH):
        tops.append(jnp.max(stat_ref[g], axis=1, keepdims=True) * to_two)
        stat_ref[g] = jnp.broadcast_to(tops[g], (stacked, HD))
        acc_ref[g] = jnp.zeros((stacked, HD), jnp.float32)
        low_ref[g] = jnp.zeros((stacked, HD), jnp.float32)

    def value_step(c, carry):
        at = pl.multiple_of(c * CHUNK, CHUNK)
        for g in range(KVH):
            v_block = kv_ref[pl.ds(at, CHUNK), wide + g * HD : wide + (g + 1) * HD]
            top = stat_ref[g]
            e = jnp.exp2(s_ref[g, c] * to_two - jnp.concatenate([top, top], axis=1))
            low_ref[g] = low_ref[g] + (e[:, :HD] + e[:, HD:])
            e_low = e.astype(jnp.bfloat16)
            e_ref[g, c] = e_low
            acc_ref[g] = acc_ref[g] + dot_nn(e_low, v_block)
        return carry

    lax.fori_loop(low, high, value_step, 0)

    for g in range(KVH):
        inverse = 1.0 / jnp.sum(low_ref[g], axis=1, keepdims=True)
        attended = acc_ref[g] * inverse
        grads = (heads_of(g_ref, g).astype(jnp.float32) * inverse).astype(jnp.bfloat16)
        inner = jnp.sum(grads.astype(jnp.float32) * attended, axis=1, keepdims=True)
        stat_ref[g] = jnp.broadcast_to(inner, (stacked, HD))
        acc_ref[g] = jnp.zeros((stacked, HD), jnp.float32)
        for r in range(GROUP):
            cols = slice((g * GROUP + r) * HD, (g * GROUP + r + 1) * HD)
            out_ref[:, cols] = attended[r * rows : (r + 1) * rows].astype(jnp.bfloat16)
            gq_ref[:, cols] = grads[r * rows : (r + 1) * rows]

    def backward_step(c, carry):
        at = pl.multiple_of(c * CHUNK, CHUNK)
        for g in range(KVH):
            keys_at, values_at = slice(g * HD, (g + 1) * HD), slice(wide + g * HD, wide + (g + 1) * HD)
            k_block = kv_ref[pl.ds(at, CHUNK), keys_at]
            v_block = kv_ref[pl.ds(at, CHUNK), values_at]
            grads = heads_of(gq_ref, g)
            inner = stat_ref[g]
            e_low = e_ref[g, c]
            grad_probs = dot_nt(grads, v_block) - jnp.concatenate([inner, inner], axis=1)
            grad_scores = (e_low.astype(jnp.float32) * grad_probs).astype(jnp.bfloat16)
            acc_ref[g] = acc_ref[g] + dot_nn(grad_scores, k_block)
            grad_k = dot_tn(grad_scores, heads_of(q_ref, g)) * scale
            grad_v = dot_tn(e_low, grads)
            gkv_ref[pl.ds(at, CHUNK), keys_at] = grad_k.astype(gkv_ref.dtype)
            gkv_ref[pl.ds(at, CHUNK), values_at] = grad_v.astype(gkv_ref.dtype)
        return carry

    lax.fori_loop(low, high, backward_step, 0)

    for g in range(KVH):
        for r in range(GROUP):
            cols = slice((g * GROUP + r) * HD, (g * GROUP + r + 1) * HD)
            gq_ref[:, cols] = (acc_ref[g, r * rows : (r + 1) * rows] * scale).astype(jnp.bfloat16)


def attend(bounds, first, queries, out_grad, kv_all):
    rows = queries.shape[0]
    all_rows = kv_all.shape[0]
    stacked = rows * GROUP
    chunks = all_rows // CHUNK
    in_vmem = pl.BlockSpec(memory_space=pltpu.VMEM)
    return pl.pallas_call(
        attend_kernel,
        out_shape=(
            jax.ShapeDtypeStruct(queries.shape, jnp.bfloat16),
            jax.ShapeDtypeStruct(queries.shape, jnp.bfloat16),
            jax.ShapeDtypeStruct(kv_all.shape, jnp.bfloat16),
        ),
        in_specs=[pl.BlockSpec(memory_space=pltpu.SMEM)] + [in_vmem] * 4,
        out_specs=(in_vmem, in_vmem, in_vmem),
        scratch_shapes=[
            pltpu.VMEM((KVH, chunks, stacked, CHUNK), jnp.float32),
            pltpu.VMEM((KVH, chunks, stacked, CHUNK), jnp.bfloat16),
            pltpu.VMEM((KVH, stacked, HD), jnp.float32),
            pltpu.VMEM((KVH, stacked, HD), jnp.float32),
            pltpu.VMEM((KVH, stacked, HD), jnp.float32),
        ],
        compiler_params=pltpu.CompilerParams(vmem_limit_bytes=56 * 1024 * 1024),
        cost_estimate=pl.CostEstimate(
            flops=6 * 2 * rows * all_rows * KVH * GROUP * HD,
            bytes_accessed=12 * 1024 * 1024,
            transcendentals=rows * all_rows * KVH * GROUP,
        ),
    )(bounds, first, queries, out_grad, kv_all)


def local(queries, keys, values, out_grad, segment_ids):
    rows = queries.shape[0]
    my_index = lax.axis_index("ctx")
    kv_all = lax.all_gather(jnp.concatenate([keys, values], axis=1), "ctx", axis=0, tiled=True)
    q_start = my_index * rows
    q_seg = lax.dynamic_slice_in_dim(segment_ids, q_start, rows, 0)
    first = jnp.sum((segment_ids[None, :] < q_seg[:, None]).astype(jnp.int32), axis=1, keepdims=True)
    bounds = jnp.stack(
        [q_start, first[0, 0] // CHUNK, (q_start + rows - 1) // CHUNK + 1, first[rows - 1, 0]]
    ).astype(jnp.int32)
    attended, grad_query, grad_kv = attend(bounds, first, queries, out_grad, kv_all)
    summed = lax.psum_scatter(grad_kv, "ctx", scatter_dimension=0, tiled=True).astype(jnp.float32)
    half = KVH * HD
    return (attended, grad_query, summed[:, :half], summed[:, half:])


def solution(mesh):
    placed = P(("dp", "ctx"), None)
    return jax.shard_map(
        local,
        mesh=mesh,
        in_specs=(placed, placed, placed, placed, P("dp")),
        out_specs=(placed, placed, placed, placed),
        check_vma=False,
    )
```

```python
import math

import jax
import jax.numpy as jnp
from jax import lax
from jax.experimental import pallas as pl
from jax.experimental.pallas import tpu as pltpu
from jax.sharding import PartitionSpec as P

KVH = 4
HD = 128
GROUP = 4
WIDE = KVH * HD
CHUNK = 256
FAR = 12
NEAR = 7
SLOTS = 14

neg_big = -1e30


def dot_nt(a, b):
    return lax.dot_general(a, b, (((1,), (1,)), ((), ())), preferred_element_type=jnp.float32)


def dot_nn(a, b):
    return lax.dot_general(a, b, (((1,), (0,)), ((), ())), preferred_element_type=jnp.float32)


def dot_tn(a, b):
    return lax.dot_general(a, b, (((0,), (0,)), ((), ())), preferred_element_type=jnp.float32)


def heads_of(ref, g):
    base = g * GROUP * HD
    return jnp.concatenate(
        [ref[:, base + r * HD : base + (r + 1) * HD] for r in range(GROUP)], axis=0
    )


def attend_kernel(bounds, first_ref, q_ref, g_ref, *rest):
    blocks = rest[: FAR + 1]
    out_ref, gq_ref = rest[FAR + 1 : FAR + 3]
    grads_out = rest[FAR + 3 : 2 * FAR + 4]
    kv_ref, gkv_ref, s_ref, e_ref, acc_ref, stat_ref, low_ref, in_sem, out_sem = rest[2 * FAR + 4 :]
    rows = q_ref.shape[0]
    stacked = rows * GROUP
    scale = 1.0 / math.sqrt(HD)
    to_two = scale / math.log(2.0)
    q_start, high, clear_from = bounds[0], bounds[1], bounds[2]

    copies = [
        pltpu.make_async_copy(block, kv_ref.at[pl.ds(r * rows, rows)], in_sem.at[r])
        for r, block in enumerate(blocks)
    ]
    for copy in copies:
        copy.start()
    kv_ref[(FAR + 1) * rows :, :] = jnp.zeros(((SLOTS - FAR - 1) * rows, 2 * WIDE), jnp.bfloat16)
    gkv_ref[...] = jnp.zeros_like(gkv_ref)
    stat_ref[...] = jnp.full(stat_ref.shape, neg_big, jnp.float32)
    first = jnp.concatenate([first_ref[...]] * GROUP, axis=0)
    q_place = q_start + jnp.bitwise_and(
        lax.broadcasted_iota(jnp.int32, (stacked, CHUNK), 0), rows - 1
    )
    lanes = lax.broadcasted_iota(jnp.int32, (stacked, CHUNK), 1)
    lanes = jnp.where(lanes < rows, lanes, lanes - 2 * rows)
    for copy in copies:
        copy.wait()

    def scores_step(c, carry):
        at = pl.multiple_of(c * CHUNK, CHUNK)
        for g in range(KVH):
            k_block = kv_ref[pl.ds(at, CHUNK), g * HD : (g + 1) * HD]
            s_ref[g, c] = dot_nt(heads_of(q_ref, g), k_block)

        @pl.when((q_start - at - rows < clear_from) | (c == 0))
        def _():
            k_place = (q_start - at) + lanes
            allowed = (k_place >= first) & (k_place <= q_place)
            for g in range(KVH):
                s_ref[g, c] = jnp.where(allowed, s_ref[g, c], neg_big)

        for g in range(KVH):
            s = s_ref[g, c]
            stat_ref[g] = jnp.maximum(stat_ref[g], jnp.maximum(s[:, :HD], s[:, HD:]))
        return carry

    lax.fori_loop(0, high, scores_step, 0)

    for g in range(KVH):
        top = jnp.max(stat_ref[g], axis=1, keepdims=True) * to_two
        stat_ref[g] = jnp.broadcast_to(top, (stacked, HD))
        acc_ref[g] = jnp.zeros((stacked, HD), jnp.float32)
        low_ref[g] = jnp.zeros((stacked, HD), jnp.float32)

    def value_step(c, carry):
        at = pl.multiple_of(c * CHUNK, CHUNK)
        for g in range(KVH):
            v_block = kv_ref[pl.ds(at, CHUNK), WIDE + g * HD : WIDE + (g + 1) * HD]
            top = stat_ref[g]
            e = jnp.exp2(s_ref[g, c] * to_two - jnp.concatenate([top, top], axis=1))
            low_ref[g] = low_ref[g] + (e[:, :HD] + e[:, HD:])
            e_low = e.astype(jnp.bfloat16)
            e_ref[g, c] = e_low
            acc_ref[g] = acc_ref[g] + dot_nn(e_low, v_block)
        return carry

    lax.fori_loop(0, high, value_step, 0)

    for g in range(KVH):
        inverse = 1.0 / jnp.sum(low_ref[g], axis=1, keepdims=True)
        attended = acc_ref[g] * inverse
        grads = (heads_of(g_ref, g).astype(jnp.float32) * inverse).astype(jnp.bfloat16)
        inner = jnp.sum(grads.astype(jnp.float32) * attended, axis=1, keepdims=True)
        stat_ref[g] = jnp.broadcast_to(inner, (stacked, HD))
        acc_ref[g] = jnp.zeros((stacked, HD), jnp.float32)
        for r in range(GROUP):
            cols = slice((g * GROUP + r) * HD, (g * GROUP + r + 1) * HD)
            out_ref[:, cols] = attended[r * rows : (r + 1) * rows].astype(jnp.bfloat16)
            gq_ref[:, cols] = grads[r * rows : (r + 1) * rows]

    def backward_step(c, carry):
        at = pl.multiple_of(c * CHUNK, CHUNK)
        for g in range(KVH):
            keys_at, values_at = slice(g * HD, (g + 1) * HD), slice(WIDE + g * HD, WIDE + (g + 1) * HD)
            k_block = kv_ref[pl.ds(at, CHUNK), keys_at]
            v_block = kv_ref[pl.ds(at, CHUNK), values_at]
            grads = heads_of(gq_ref, g)
            inner = stat_ref[g]
            e_low = e_ref[g, c]
            grad_probs = dot_nt(grads, v_block) - jnp.concatenate([inner, inner], axis=1)
            grad_scores = (e_low.astype(jnp.float32) * grad_probs).astype(jnp.bfloat16)
            acc_ref[g] = acc_ref[g] + dot_nn(grad_scores, k_block)
            grad_k = dot_tn(grad_scores, heads_of(q_ref, g)) * scale
            grad_v = dot_tn(e_low, grads)
            gkv_ref[pl.ds(at, CHUNK), keys_at] = grad_k.astype(gkv_ref.dtype)
            gkv_ref[pl.ds(at, CHUNK), values_at] = grad_v.astype(gkv_ref.dtype)
        return carry

    lax.fori_loop(0, high, backward_step, 0)

    copies = [
        pltpu.make_async_copy(gkv_ref.at[pl.ds(r * rows, rows)], grad, out_sem.at[r])
        for r, grad in enumerate(grads_out)
    ]
    for copy in copies:
        copy.start()
    for g in range(KVH):
        for r in range(GROUP):
            cols = slice((g * GROUP + r) * HD, (g * GROUP + r + 1) * HD)
            gq_ref[:, cols] = (acc_ref[g, r * rows : (r + 1) * rows] * scale).astype(jnp.bfloat16)
    for copy in copies:
        copy.wait()


def attend(bounds, first, queries, out_grad, blocks):
    rows = queries.shape[0]
    stacked = rows * GROUP
    chunks = SLOTS * rows // CHUNK
    in_vmem = pl.BlockSpec(memory_space=pltpu.VMEM)
    anywhere = pl.BlockSpec(memory_space=pl.ANY)
    results = pl.pallas_call(
        attend_kernel,
        out_shape=[jax.ShapeDtypeStruct(queries.shape, jnp.bfloat16)] * 2
        + [jax.ShapeDtypeStruct(blocks[0].shape, jnp.bfloat16)] * (FAR + 1),
        in_specs=[pl.BlockSpec(memory_space=pltpu.SMEM)] + [in_vmem] * 3 + [anywhere] * (FAR + 1),
        out_specs=[in_vmem] * 2 + [anywhere] * (FAR + 1),
        scratch_shapes=[
            pltpu.VMEM((SLOTS * rows, 2 * WIDE), jnp.bfloat16),
            pltpu.VMEM((SLOTS * rows, 2 * WIDE), jnp.bfloat16),
            pltpu.VMEM((KVH, chunks, stacked, CHUNK), jnp.float32),
            pltpu.VMEM((KVH, chunks, stacked, CHUNK), jnp.bfloat16),
            pltpu.VMEM((KVH, stacked, HD), jnp.float32),
            pltpu.VMEM((KVH, stacked, HD), jnp.float32),
            pltpu.VMEM((KVH, stacked, HD), jnp.float32),
            pltpu.SemaphoreType.DMA((FAR + 1,)),
            pltpu.SemaphoreType.DMA((FAR + 1,)),
        ],
        compiler_params=pltpu.CompilerParams(vmem_limit_bytes=56 * 1024 * 1024),
        cost_estimate=pl.CostEstimate(
            flops=6 * 2 * rows * SLOTS * rows * KVH * GROUP * HD,
            bytes_accessed=12 * 1024 * 1024,
            transcendentals=rows * SLOTS * rows * KVH * GROUP,
        ),
    )(bounds, first, queries, out_grad, *blocks)
    return results[0], results[1], results[2:]


def send(x, pairs):
    return lax.ppermute(x, "ctx", pairs)


def gather_blocks(own, count):
    back = {0: own}
    wrapped = range(count - NEAR - 1)
    for step in range(1, max(NEAR, FAR - NEAR) + 1):
        if step <= NEAR:
            back[step] = send(back[step - 1], [(j, j + 1) for j in range(step - 1, count - 1)])
        r = FAR + 1 - step
        if r > NEAR:
            by = count - FAR if step == 1 else 1
            back[r] = send(
                own if step == 1 else back[r + 1],
                [((b + r + by) % count, (b + r) % count) for b in wrapped],
            )
    return [back[r] for r in range(FAR + 1)]


def add_low(a, b):
    return (a.astype(jnp.float32) + b.astype(jnp.float32)).astype(jnp.bfloat16)


def return_sums(terms, count):
    wrapped = range(count - NEAR - 1)
    near, far = terms[NEAR], terms[NEAR + 1]
    for step in range(1, max(NEAR, FAR - NEAR) + 1):
        r = NEAR + step
        if r <= FAR:
            by = count - FAR if r == FAR else 1
            far = send(far, [((b + r) % count, (b + r + by) % count) for b in wrapped])
            if r < FAR:
                far = add_low(far, terms[r + 1])
        if step <= NEAR:
            r = NEAR + 1 - step
            near = send(near, [(j, j - 1) for j in range(r, count)])
            if r > 1:
                near = add_low(near, terms[r - 1])
    return near, far


def local(queries, keys, values, out_grad, segment_ids):
    rows = queries.shape[0]
    count = lax.axis_size("ctx")
    q_start = lax.axis_index("ctx") * rows
    blocks = gather_blocks(jnp.concatenate([keys, values], axis=1), count)
    q_seg = lax.dynamic_slice_in_dim(segment_ids, q_start, rows, 0)
    first = jnp.sum((segment_ids[None, :] < q_seg[:, None]).astype(jnp.int32), axis=1, keepdims=True)
    high = (q_start + rows - first[0, 0] + CHUNK - 1) // CHUNK
    bounds = jnp.stack([q_start, high, first[rows - 1, 0]]).astype(jnp.int32)
    attended, grad_query, terms = attend(bounds, first, queries, out_grad, blocks)
    near, far = return_sums(terms, count)
    summed = near.astype(jnp.float32) + far.astype(jnp.float32) + terms[0].astype(jnp.float32)
    return (attended, grad_query, summed[:, :WIDE], summed[:, WIDE:])


def solution(mesh):
    placed = P(("dp", "ctx"), None)
    return jax.shard_map(
        local,
        mesh=mesh,
        in_specs=(placed, placed, placed, placed, P("dp")),
        out_specs=(placed, placed, placed, placed),
        check_vma=False,
    )
```

```python
import functools
import math

import jax
import jax.numpy as jnp
from jax import lax
from jax.experimental import pallas as pl
from jax.experimental.pallas import tpu as pltpu
from jax.sharding import PartitionSpec as P

KVH = 4
HD = 128
GROUP = 4
WIDE = KVH * HD
FAR = 12
STEPS = 7
LANES = GROUP * 128
SCALE = 1.0 / math.sqrt(HD)
TO_TWO = SCALE / math.log(2.0)

neg_big = -1e30


def dot_nt(a, b):
    return lax.dot_general(a, b, (((1,), (1,)), ((), ())), preferred_element_type=jnp.float32)


def dot_nn(a, b):
    return lax.dot_general(a, b, (((1,), (0,)), ((), ())), preferred_element_type=jnp.float32)


def dot_tn(a, b):
    return lax.dot_general(a, b, (((0,), (0,)), ((), ())), preferred_element_type=jnp.float32)


def heads_of(ref, g):
    base = g * GROUP * HD
    return jnp.concatenate(
        [ref[:, base + r * HD : base + (r + 1) * HD] for r in range(GROUP)], axis=0
    )


def put_heads(ref, g, turned):
    flat = turned.T
    rows = ref.shape[0]
    for r in range(GROUP):
        cols = slice((g * GROUP + r) * HD, (g * GROUP + r + 1) * HD)
        ref[:, cols] = flat[r * rows : (r + 1) * rows].astype(ref.dtype)


def keys_of(blocks, g):
    return jnp.concatenate([b[:, g * HD : (g + 1) * HD] for b in blocks], axis=0)


def values_of(blocks, g):
    return jnp.concatenate([b[:, WIDE + g * HD : WIDE + (g + 1) * HD] for b in blocks], axis=0)


def allowed_keys(scal, first_ref, backs, rows):
    q_start = scal[0]
    first = jnp.concatenate([first_ref[...]] * GROUP, axis=1)
    within = lax.broadcasted_iota(jnp.int32, (rows, LANES), 0)
    parts = []
    for back in backs:
        place = (q_start - back * rows) + within
        seen = place >= first
        if isinstance(back, int) and back == 0:
            lanes = lax.broadcasted_iota(jnp.int32, (rows, LANES), 1)
            seen = seen & (within <= jnp.bitwise_and(lanes, rows - 1))
        parts.append(seen)
    return jnp.concatenate(parts, axis=0)


def forward_part(scal, first_ref, q_ref, blocks, backs, top_ref, sum_ref, acc_ref):
    allowed = allowed_keys(scal, first_ref, backs, q_ref.shape[0])
    for g in range(KVH):
        s = dot_nt(keys_of(blocks, g), heads_of(q_ref, g)) * TO_TWO
        s = jnp.where(allowed, s, neg_big)
        top = top_ref[g]
        new_top = jnp.maximum(top, jnp.max(s, axis=0, keepdims=True))
        e = jnp.exp2(s - new_top)
        shrink = jnp.exp2(top - new_top)
        top_ref[g] = new_top
        sum_ref[g] = sum_ref[g] * shrink + jnp.sum(e, axis=0, keepdims=True)
        acc_ref[g] = acc_ref[g] * shrink + dot_tn(values_of(blocks, g), e.astype(jnp.bfloat16))


def backward_part(scal, first_ref, q_ref, g_ref, blocks, backs, log_ref, inner_ref, acc_ref, outs):
    rows = q_ref.shape[0]
    allowed = allowed_keys(scal, first_ref, backs, rows)
    for g in range(KVH):
        k, v = keys_of(blocks, g), values_of(blocks, g)
        q, grads = heads_of(q_ref, g), heads_of(g_ref, g)
        s = dot_nt(k, q) * TO_TWO - log_ref[g]
        probs = jnp.exp2(jnp.where(allowed, s, neg_big))
        grad_probs = dot_nt(v, grads)
        grad_scores = (probs * (grad_probs - inner_ref[g])).astype(jnp.bfloat16)
        acc_ref[g] = acc_ref[g] + dot_tn(k, grad_scores)
        grad_k = dot_nn(grad_scores, q) * SCALE
        grad_v = dot_nn(probs.astype(jnp.bfloat16), grads)
        for i, out in enumerate(outs):
            part = slice(i * rows, (i + 1) * rows)
            out[:, g * HD : (g + 1) * HD] = grad_k[part].astype(out.dtype)
            out[:, WIDE + g * HD : WIDE + (g + 1) * HD] = grad_v[part].astype(out.dtype)


def backs_of(scal, step):
    near, far = step, 15 - step
    odd = scal[2] == 1
    return [jnp.where(odd, far, near), jnp.where(odd, near, far)]


class Near:
    def __init__(self, scal, a, b):
        self.even, self.a, self.b = scal[2] == 0, a, b

    def __getitem__(self, at):
        return jnp.where(self.even, self.a[at], self.b[at])


def first_kernel(scal, first_ref, q_ref, g_ref, own, a1, b1, a2, b2, top, total, acc, turned):
    rows = q_ref.shape[0]
    top[...] = jnp.full(top.shape, neg_big, jnp.float32)
    total[...] = jnp.zeros(total.shape, jnp.float32)
    acc[...] = jnp.zeros(acc.shape, jnp.float32)
    forward_part(scal, first_ref, q_ref, [own], [0], top, total, acc)

    @pl.when(scal[1] >= 1)
    def _():
        near = [Near(scal, a1, b1), Near(scal, a2, b2)]
        forward_part(scal, first_ref, q_ref, near, [1, 2], top, total, acc)

    for g in range(KVH):
        turned[g] = heads_of(g_ref, g).astype(jnp.float32).T


def more_kernel(steps, scal, first_ref, q_ref, top_in, total_in, acc_in, *rest):
    blocks, (top, total, acc) = rest[: 2 * len(steps)], rest[2 * len(steps) :]
    top[...] = top_in[...]
    total[...] = total_in[...]
    acc[...] = acc_in[...]
    for i, step in enumerate(steps):

        @pl.when(scal[1] >= step)
        def _(i=i, step=step):
            pair = blocks[2 * i : 2 * i + 2]
            forward_part(scal, first_ref, q_ref, pair, backs_of(scal, step), top, total, acc)


def middle_kernel(
    scal, first_ref, q_ref, g_ref, turned, top_in, total_in, acc_in, a, b,
    out_ref, log_ref, inner_ref, gq_acc, term_a, term_b, acc,
):
    log_ref[...] = top_in[...]
    inner_ref[...] = total_in[...]
    acc[...] = acc_in[...]

    @pl.when(scal[1] >= STEPS)
    def _():
        backs = backs_of(scal, STEPS)
        forward_part(scal, first_ref, q_ref, [a, b], backs, log_ref, inner_ref, acc)

    for g in range(KVH):
        total = inner_ref[g]
        attended = acc[g] * (1.0 / total)
        log_ref[g] = log_ref[g] + jnp.log2(total)
        inner_ref[g] = jnp.sum(attended * turned[g], axis=0, keepdims=True)
        put_heads(out_ref, g, attended)
    gq_acc[...] = jnp.zeros(gq_acc.shape, jnp.float32)
    back_step(STEPS, scal, first_ref, q_ref, g_ref, a, b, log_ref, inner_ref, gq_acc, term_a, term_b)


def back_step(step, scal, first_ref, q_ref, g_ref, a, b, log_ref, inner_ref, acc, term_a, term_b):
    @pl.when(scal[1] >= step)
    def _():
        backs = backs_of(scal, step)
        backward_part(
            scal, first_ref, q_ref, g_ref, [a, b], backs, log_ref, inner_ref, acc, [term_a, term_b]
        )

    @pl.when(scal[1] < step)
    def _():
        term_a[...] = jnp.zeros(term_a.shape, term_a.dtype)
        term_b[...] = jnp.zeros(term_b.shape, term_b.dtype)


def back_kernel(
    step, scal, first_ref, q_ref, g_ref, log_ref, inner_ref, acc_in, a, b, acc, term_a, term_b
):
    acc[...] = acc_in[...]
    back_step(step, scal, first_ref, q_ref, g_ref, a, b, log_ref, inner_ref, acc, term_a, term_b)


def last_kernel(
    scal, first_ref, q_ref, g_ref, log_ref, inner_ref, acc_in, own, a1, b1, a2, b2,
    gq_ref, term_0, term_1, term_2, acc,
):
    acc[...] = acc_in[...]
    backward_part(
        scal, first_ref, q_ref, g_ref, [own], [0], log_ref, inner_ref, acc, [term_0]
    )

    @pl.when(scal[1] >= 1)
    def _():
        near = [Near(scal, a1, b1), Near(scal, a2, b2)]
        backward_part(
            scal, first_ref, q_ref, g_ref, near, [1, 2], log_ref, inner_ref, acc, [term_1, term_2]
        )

    @pl.when(scal[1] < 1)
    def _():
        term_1[...] = jnp.zeros(term_1.shape, term_1.dtype)
        term_2[...] = jnp.zeros(term_2.shape, term_2.dtype)

    for g in range(KVH):
        put_heads(gq_ref, g, acc[g] * SCALE)


ROW = jax.ShapeDtypeStruct((KVH, 1, LANES), jnp.float32)
TURNED = jax.ShapeDtypeStruct((KVH, HD, LANES), jnp.float32)


def call(kernel, outs, work, scal, *operands, scratch=()):
    in_vmem = pl.BlockSpec(memory_space=pltpu.VMEM)
    return pl.pallas_call(
        kernel,
        out_shape=outs,
        in_specs=[pl.BlockSpec(memory_space=pltpu.SMEM)] + [in_vmem] * len(operands),
        out_specs=[in_vmem] * len(outs),
        scratch_shapes=list(scratch),
        compiler_params=pltpu.CompilerParams(vmem_limit_bytes=24 * 1024 * 1024),
        cost_estimate=pl.CostEstimate(
            flops=int(work * 1.0e9), bytes_accessed=4 * 1024 * 1024, transcendentals=1 << 20
        ),
    )(scal, *operands)


def both_ways(x, near_pairs, far_pairs, flip):
    windows, count = lax.axis_size("dp"), lax.axis_size("ctx")
    pairs = []
    for window in range(windows):
        chosen = near_pairs if (window + flip) % 2 == 0 else far_pairs
        pairs += [(window * count + i, window * count + j) for i, j in chosen]
    return lax.ppermute(x, ("dp", "ctx"), pairs)


def gather_pairs(step, count):
    near = [(j, j + 1) for j in range(step - 1, count - 1)]
    blocks = range(count - STEPS - 1)
    start = 0 if step == 1 else step
    far = [((b - start) % count, (b - step - 1) % count) for b in blocks]
    return near, far


def return_pairs(step, count):
    near = [(j, j - 1) for j in range(STEPS + 1 - step, count)]
    blocks = range(count - STEPS - 1)
    end = STEPS + 1 + step if step < STEPS else count
    far = [((b + STEPS + step) % count, (b + end) % count) for b in blocks]
    return near, far


def add_low(a, b):
    return (a.astype(jnp.float32) + b.astype(jnp.float32)).astype(jnp.bfloat16)


def local(queries, keys, values, out_grad, segment_ids):
    rows = queries.shape[0]
    count = lax.axis_size("ctx")
    odd = lax.rem(lax.axis_index("dp"), 2)
    q_start = lax.axis_index("ctx") * rows
    own = jnp.concatenate([keys, values], axis=1)
    q_seg = lax.dynamic_slice_in_dim(segment_ids, q_start, rows, 0)
    first = jnp.sum((segment_ids[:, None] < q_seg[None, :]).astype(jnp.int32), axis=0, keepdims=True)
    scal = jnp.stack([q_start, (q_start - first[0, 0] + rows - 1) // rows, odd]).astype(jnp.int32)

    block = jax.ShapeDtypeStruct(own.shape, jnp.bfloat16)
    wide = jax.ShapeDtypeStruct(queries.shape, jnp.bfloat16)
    a, b, tops = [own], [own], {}
    for step in range(1, STEPS + 1):
        pairs = gather_pairs(step, count)
        to_a = a[-1]
        if step in (5, 7):
            to_a, _ = lax.optimization_barrier((to_a, tops[step - 3]))
        a.append(both_ways(to_a, *pairs, 0))
        b.append(both_ways(b[-1], *pairs, 1))
        if step == 2:
            top, total, acc, turned = call(
                first_kernel, [ROW, ROW, TURNED, TURNED], 0.8,
                scal, first, queries, out_grad, own, a[1], b[1], a[2], b[2],
            )
        elif step in (4, 6):
            pairs = [x for i in (step - 1, step) for x in (a[i], b[i])]
            top, total, acc = call(
                functools.partial(more_kernel, (step - 1, step)), [ROW, ROW, TURNED], 1.0,
                scal, first, queries, top, total, acc, *pairs,
            )
        tops[step] = top if step > 1 else None
    attended, log_total, inner, acc, term_a, term_b = call(
        middle_kernel, [wide, ROW, ROW, TURNED, block, block], 1.5,
        scal, first, queries, out_grad, turned, top, total, acc, a[STEPS], b[STEPS],
        scratch=[pltpu.VMEM((KVH, HD, LANES), jnp.float32)],
    )

    sum_a, sum_b = term_a, term_b
    for step in range(1, STEPS + 1):
        pairs = return_pairs(step, count)
        sum_a = both_ways(sum_a, *pairs, 0)
        sum_b = both_ways(sum_b, *pairs, 1)
        back = STEPS - step
        if back >= 3:
            acc, term_a, term_b = call(
                functools.partial(back_kernel, back), [TURNED, block, block], 1.2,
                scal, first, queries, out_grad, log_total, inner, acc, a[back], b[back],
            )
            sum_a, sum_b = add_low(sum_a, term_a), add_low(sum_b, term_b)
        elif back >= 1:
            if back == 2:
                grad_query, term_0, term_1, term_2 = call(
                    last_kernel, [wide, jax.ShapeDtypeStruct(own.shape, jnp.float32), block, block], 2.0,
                    scal, first, queries, out_grad, log_total, inner, acc, own, a[1], b[1], a[2], b[2],
                    scratch=[pltpu.VMEM((KVH, HD, LANES), jnp.float32)],
                )
            term = term_2 if back == 2 else term_1
            nothing = jnp.zeros_like(term)
            sum_a = add_low(sum_a, jnp.where(odd == 0, term, nothing))
            sum_b = add_low(sum_b, jnp.where(odd == 1, term, nothing))
    summed = sum_a.astype(jnp.float32) + sum_b.astype(jnp.float32) + term_0
    return (attended, grad_query, summed[:, :WIDE], summed[:, WIDE:])


def solution(mesh):
    placed = P(("dp", "ctx"), None)
    return jax.shard_map(
        local,
        mesh=mesh,
        in_specs=(placed, placed, placed, placed, P("dp")),
        out_specs=(placed, placed, placed, placed),
        check_vma=False,
    )
```

```python
import functools
import math

import jax
import jax.numpy as jnp
from jax import lax
from jax.experimental import pallas as pl
from jax.experimental.pallas import tpu as pltpu
from jax.sharding import PartitionSpec as P

KVH = 4
HD = 128
GROUP = 4
WIDE = KVH * HD
FAR = 12
STEPS = 7
LANES = GROUP * 128
SCALE = 1.0 / math.sqrt(HD)
TO_TWO = SCALE / math.log(2.0)

neg_big = -1e30


def dot_nt(a, b):
    return lax.dot_general(a, b, (((1,), (1,)), ((), ())), preferred_element_type=jnp.float32)


def dot_nn(a, b):
    return lax.dot_general(a, b, (((1,), (0,)), ((), ())), preferred_element_type=jnp.float32)


def dot_tn(a, b):
    return lax.dot_general(a, b, (((0,), (0,)), ((), ())), preferred_element_type=jnp.float32)


def heads_of(ref, g):
    base = g * GROUP * HD
    return jnp.concatenate(
        [ref[:, base + r * HD : base + (r + 1) * HD] for r in range(GROUP)], axis=0
    )


def put_heads(ref, g, turned):
    flat = turned.T
    rows = ref.shape[0]
    for r in range(GROUP):
        cols = slice((g * GROUP + r) * HD, (g * GROUP + r + 1) * HD)
        ref[:, cols] = flat[r * rows : (r + 1) * rows].astype(ref.dtype)


def keys_of(blocks, g):
    return jnp.concatenate([k[:, g * HD : (g + 1) * HD] for k, _ in blocks], axis=0)


def values_of(blocks, g):
    return jnp.concatenate([v[:, g * HD : (g + 1) * HD] for _, v in blocks], axis=0)


def allowed_keys(scal, first_ref, backs, rows):
    q_start = scal[0]
    first = jnp.concatenate([first_ref[...]] * GROUP, axis=1)
    within = lax.broadcasted_iota(jnp.int32, (rows, LANES), 0)
    parts = []
    for back in backs:
        place = (q_start - back * rows) + within
        seen = place >= first
        if isinstance(back, int) and back == 0:
            lanes = lax.broadcasted_iota(jnp.int32, (rows, LANES), 1)
            seen = seen & (within <= jnp.bitwise_and(lanes, rows - 1))
        parts.append(seen)
    return jnp.concatenate(parts, axis=0)


def forward_part(scal, first_ref, q_ref, blocks, backs, top_ref, sum_ref, acc_ref):
    allowed = allowed_keys(scal, first_ref, backs, q_ref.shape[0])
    for g in range(KVH):
        s = dot_nt(keys_of(blocks, g), heads_of(q_ref, g)) * TO_TWO
        s = jnp.where(allowed, s, neg_big)
        top = top_ref[g]
        new_top = jnp.maximum(top, jnp.max(s, axis=0, keepdims=True))
        e = jnp.exp2(s - new_top)
        shrink = jnp.exp2(top - new_top)
        top_ref[g] = new_top
        sum_ref[g] = sum_ref[g] * shrink + jnp.sum(e, axis=0, keepdims=True)
        acc_ref[g] = acc_ref[g] * shrink + dot_tn(values_of(blocks, g), e.astype(jnp.bfloat16))


def backward_part(scal, first_ref, q_ref, g_ref, blocks, backs, log_ref, inner_ref, acc_ref, outs):
    rows = q_ref.shape[0]
    allowed = allowed_keys(scal, first_ref, backs, rows)
    for g in range(KVH):
        k, v = keys_of(blocks, g), values_of(blocks, g)
        q, grads = heads_of(q_ref, g), heads_of(g_ref, g)
        s = dot_nt(k, q) * TO_TWO - log_ref[g]
        probs = jnp.exp2(jnp.where(allowed, s, neg_big))
        grad_probs = dot_nt(v, grads)
        grad_scores = (probs * (grad_probs - inner_ref[g])).astype(jnp.bfloat16)
        acc_ref[g] = acc_ref[g] + dot_tn(k, grad_scores)
        grad_k = dot_nn(grad_scores, q) * SCALE
        grad_v = dot_nn(probs.astype(jnp.bfloat16), grads)
        cols = slice(g * HD, (g + 1) * HD)
        for i, (out_k, out_v) in enumerate(outs):
            part = slice(i * rows, (i + 1) * rows)
            out_k[:, cols] = grad_k[part].astype(out_k.dtype)
            out_v[:, cols] = grad_v[part].astype(out_v.dtype)


def backs_of(scal, step):
    near, far = step, 15 - step
    odd = scal[2] == 1
    return [jnp.where(odd, far, near), jnp.where(odd, near, far)]


class Near:
    def __init__(self, scal, a, b):
        self.even, self.a, self.b = scal[2] == 0, a, b

    def __getitem__(self, at):
        return jnp.where(self.even, self.a[at], self.b[at])


def near_blocks(scal, arrays):
    ak1, av1, bk1, bv1, ak2, av2, bk2, bv2 = arrays
    return [
        (Near(scal, ak1, bk1), Near(scal, av1, bv1)),
        (Near(scal, ak2, bk2), Near(scal, av2, bv2)),
    ]


def first_kernel(scal, first_ref, q_ref, g_ref, own_k, own_v, *rest):
    top, total, acc, turned = rest[8:]
    rows = q_ref.shape[0]
    top[...] = jnp.full(top.shape, neg_big, jnp.float32)
    total[...] = jnp.zeros(total.shape, jnp.float32)
    acc[...] = jnp.zeros(acc.shape, jnp.float32)
    forward_part(scal, first_ref, q_ref, [(own_k, own_v)], [0], top, total, acc)

    @pl.when(scal[1] >= 1)
    def _():
        near = near_blocks(scal, rest[:8])
        forward_part(scal, first_ref, q_ref, near, [1, 2], top, total, acc)

    for g in range(KVH):
        turned[g] = heads_of(g_ref, g).astype(jnp.float32).T


def more_kernel(steps, scal, first_ref, q_ref, top_in, total_in, acc_in, *rest):
    blocks, (top, total, acc) = rest[: 4 * len(steps)], rest[4 * len(steps) :]
    top[...] = top_in[...]
    total[...] = total_in[...]
    acc[...] = acc_in[...]
    for i, step in enumerate(steps):

        @pl.when(scal[1] >= step)
        def _(i=i, step=step):
            ak, av, bk, bv = blocks[4 * i : 4 * i + 4]
            pair = [(ak, av), (bk, bv)]
            forward_part(scal, first_ref, q_ref, pair, backs_of(scal, step), top, total, acc)


def middle_kernel(
    scal, first_ref, q_ref, g_ref, turned, top_in, total_in, acc_in, ak, av, bk, bv,
    out_ref, log_ref, inner_ref, gq_acc, tak, tav, tbk, tbv, acc,
):
    log_ref[...] = top_in[...]
    inner_ref[...] = total_in[...]
    acc[...] = acc_in[...]

    @pl.when(scal[1] >= STEPS)
    def _():
        backs = backs_of(scal, STEPS)
        forward_part(scal, first_ref, q_ref, [(ak, av), (bk, bv)], backs, log_ref, inner_ref, acc)

    for g in range(KVH):
        total = inner_ref[g]
        attended = acc[g] * (1.0 / total)
        log_ref[g] = log_ref[g] + jnp.log2(total)
        inner_ref[g] = jnp.sum(attended * turned[g], axis=0, keepdims=True)
        put_heads(out_ref, g, attended)
    gq_acc[...] = jnp.zeros(gq_acc.shape, jnp.float32)
    blocks, terms = [(ak, av), (bk, bv)], [(tak, tav), (tbk, tbv)]
    back_step(STEPS, scal, first_ref, q_ref, g_ref, blocks, log_ref, inner_ref, gq_acc, terms)


def clear(terms):
    for pair in terms:
        for term in pair:
            term[...] = jnp.zeros(term.shape, term.dtype)


def back_step(step, scal, first_ref, q_ref, g_ref, blocks, log_ref, inner_ref, acc, terms):
    @pl.when(scal[1] >= step)
    def _():
        backs = backs_of(scal, step)
        backward_part(
            scal, first_ref, q_ref, g_ref, blocks, backs, log_ref, inner_ref, acc, terms
        )

    @pl.when(scal[1] < step)
    def _():
        clear(terms)


def back_kernel(
    step, scal, first_ref, q_ref, g_ref, log_ref, inner_ref, acc_in, ak, av, bk, bv,
    acc, tak, tav, tbk, tbv,
):
    acc[...] = acc_in[...]
    blocks, terms = [(ak, av), (bk, bv)], [(tak, tav), (tbk, tbv)]
    back_step(step, scal, first_ref, q_ref, g_ref, blocks, log_ref, inner_ref, acc, terms)


def last_kernel(scal, first_ref, q_ref, g_ref, log_ref, inner_ref, acc_in, own_k, own_v, *rest):
    gq_ref, tk0, tv0, tk1, tv1, tk2, tv2, acc = rest[8:]
    acc[...] = acc_in[...]
    backward_part(
        scal, first_ref, q_ref, g_ref, [(own_k, own_v)], [0], log_ref, inner_ref, acc, [(tk0, tv0)]
    )
    terms = [(tk1, tv1), (tk2, tv2)]

    @pl.when(scal[1] >= 1)
    def _():
        near = near_blocks(scal, rest[:8])
        backward_part(
            scal, first_ref, q_ref, g_ref, near, [1, 2], log_ref, inner_ref, acc, terms
        )

    @pl.when(scal[1] < 1)
    def _():
        clear(terms)

    for g in range(KVH):
        put_heads(gq_ref, g, acc[g] * SCALE)


ROW = jax.ShapeDtypeStruct((KVH, 1, LANES), jnp.float32)
TURNED = jax.ShapeDtypeStruct((KVH, HD, LANES), jnp.float32)


def call(kernel, outs, work, scal, *operands, scratch=()):
    in_vmem = pl.BlockSpec(memory_space=pltpu.VMEM)
    return pl.pallas_call(
        kernel,
        out_shape=outs,
        in_specs=[pl.BlockSpec(memory_space=pltpu.SMEM)] + [in_vmem] * len(operands),
        out_specs=[in_vmem] * len(outs),
        scratch_shapes=list(scratch),
        compiler_params=pltpu.CompilerParams(vmem_limit_bytes=24 * 1024 * 1024),
        cost_estimate=pl.CostEstimate(
            flops=int(work * 1.0e9), bytes_accessed=4 * 1024 * 1024, transcendentals=1 << 20
        ),
    )(scal, *operands)


def both_ways(x, near_pairs, far_pairs, flip):
    windows, count = lax.axis_size("dp"), lax.axis_size("ctx")
    pairs = []
    for window in range(windows):
        chosen = near_pairs if (window + flip) % 2 == 0 else far_pairs
        pairs += [(window * count + i, window * count + j) for i, j in chosen]
    return lax.ppermute(x, ("dp", "ctx"), pairs)


def gather_pairs(step, count):
    near = [(j, j + 1) for j in range(step - 1, count - 1)]
    blocks = range(count - STEPS - 1)
    start = 0 if step == 1 else step
    far = [((b - start) % count, (b - step - 1) % count) for b in blocks]
    return near, far


def return_pairs(step, count):
    near = [(j, j - 1) for j in range(STEPS + 1 - step, count)]
    blocks = range(count - STEPS - 1)
    end = STEPS + 1 + step if step < STEPS else count
    far = [((b + STEPS + step) % count, (b + end) % count) for b in blocks]
    return near, far


def add_low(a, b):
    return (a.astype(jnp.float32) + b.astype(jnp.float32)).astype(jnp.bfloat16)


def step_all(held, pairs):
    return [both_ways(x, *pairs, i // 2) for i, x in enumerate(held)]


def local(queries, keys, values, out_grad, segment_ids):
    rows = queries.shape[0]
    count = lax.axis_size("ctx")
    odd = lax.rem(lax.axis_index("dp"), 2)
    q_start = lax.axis_index("ctx") * rows
    q_seg = lax.dynamic_slice_in_dim(segment_ids, q_start, rows, 0)
    first = jnp.sum((segment_ids[:, None] < q_seg[None, :]).astype(jnp.int32), axis=0, keepdims=True)
    scal = jnp.stack([q_start, (q_start - first[0, 0] + rows - 1) // rows, odd]).astype(jnp.int32)

    block = jax.ShapeDtypeStruct(keys.shape, jnp.bfloat16)
    exact = jax.ShapeDtypeStruct(keys.shape, jnp.float32)
    wide = jax.ShapeDtypeStruct(queries.shape, jnp.bfloat16)
    chains, tops = [[keys, values, keys, values]], {}
    for step in range(1, STEPS + 1):
        held = list(chains[-1])
        if step in (5, 7):
            held[0], _ = lax.optimization_barrier((held[0], tops[step - 3]))
        chains.append(step_all(held, gather_pairs(step, count)))
        if step == 2:
            top, total, acc, turned = call(
                first_kernel, [ROW, ROW, TURNED, TURNED], 0.8,
                scal, first, queries, out_grad, keys, values, *chains[1], *chains[2],
            )
        elif step in (4, 6):
            top, total, acc = call(
                functools.partial(more_kernel, (step - 1, step)), [ROW, ROW, TURNED], 1.0,
                scal, first, queries, top, total, acc, *chains[step - 1], *chains[step],
            )
        tops[step] = top if step > 1 else None
    attended, log_total, inner, acc, *terms = call(
        middle_kernel, [wide, ROW, ROW, TURNED] + [block] * 4, 1.5,
        scal, first, queries, out_grad, turned, top, total, acc, *chains[STEPS],
        scratch=[pltpu.VMEM((KVH, HD, LANES), jnp.float32)],
    )

    sums = terms
    for step in range(1, STEPS + 1):
        back = STEPS - step
        if step > 1 and back >= 2:
            acc, _ = lax.optimization_barrier((acc, sums[0]))
        sums = step_all(sums, return_pairs(step, count))
        if back >= 3:
            acc, *terms = call(
                functools.partial(back_kernel, back), [TURNED] + [block] * 4, 1.2,
                scal, first, queries, out_grad, log_total, inner, acc, *chains[back],
            )
            sums = [add_low(x, term) for x, term in zip(sums, terms)]
        elif back >= 1:
            if back == 2:
                grad_query, own_k, own_v, *terms = call(
                    last_kernel, [wide, exact, exact] + [block] * 4, 2.0,
                    scal, first, queries, out_grad, log_total, inner, acc,
                    keys, values, *chains[1], *chains[2],
                    scratch=[pltpu.VMEM((KVH, HD, LANES), jnp.float32)],
                )
            near = terms[2 * back - 2 : 2 * back]
            sums = [
                add_low(x, jnp.where(odd == i // 2, near[i % 2], jnp.zeros_like(x)))
                for i, x in enumerate(sums)
            ]
    a_k, a_v, b_k, b_v = [x.astype(jnp.float32) for x in sums]
    return (attended, grad_query, a_k + b_k + own_k, a_v + b_v + own_v)


def solution(mesh):
    placed = P(("dp", "ctx"), None)
    return jax.shard_map(
        local,
        mesh=mesh,
        in_specs=(placed, placed, placed, placed, P("dp")),
        out_specs=(placed, placed, placed, placed),
        check_vma=False,
    )
```

```python
import functools
import math

import jax
import jax.numpy as jnp
from jax import lax
from jax.experimental import pallas as pl
from jax.experimental.pallas import tpu as pltpu
from jax.sharding import PartitionSpec as P

KVH = 4
HD = 128
GROUP = 4
WIDE = KVH * HD
FAR = 12
STEPS = 7
LANES = GROUP * 128
SCALE = 1.0 / math.sqrt(HD)
TO_TWO = SCALE / math.log(2.0)

neg_big = -1e30


def dot_nt(a, b):
    return lax.dot_general(a, b, (((1,), (1,)), ((), ())), preferred_element_type=jnp.float32)


def dot_nn(a, b):
    return lax.dot_general(a, b, (((1,), (0,)), ((), ())), preferred_element_type=jnp.float32)


def dot_tn(a, b):
    return lax.dot_general(a, b, (((0,), (0,)), ((), ())), preferred_element_type=jnp.float32)


def heads_of(ref, g):
    base = g * GROUP * HD
    return jnp.concatenate(
        [ref[:, base + r * HD : base + (r + 1) * HD] for r in range(GROUP)], axis=0
    )


def put_heads(ref, g, turned):
    flat = turned.T
    rows = ref.shape[0]
    for r in range(GROUP):
        cols = slice((g * GROUP + r) * HD, (g * GROUP + r + 1) * HD)
        ref[:, cols] = flat[r * rows : (r + 1) * rows].astype(ref.dtype)


def keys_of(blocks, g):
    return jnp.concatenate([b[:, g * HD : (g + 1) * HD] for b in blocks], axis=0)


def values_of(blocks, g):
    return jnp.concatenate([b[:, WIDE + g * HD : WIDE + (g + 1) * HD] for b in blocks], axis=0)


def allowed_keys(scal, first_ref, backs, rows):
    q_start = scal[0]
    first = jnp.concatenate([first_ref[...]] * GROUP, axis=1)
    within = lax.broadcasted_iota(jnp.int32, (rows, LANES), 0)
    parts = []
    for back in backs:
        place = (q_start - back * rows) + within
        seen = place >= first
        if isinstance(back, int) and back == 0:
            lanes = lax.broadcasted_iota(jnp.int32, (rows, LANES), 1)
            seen = seen & (within <= jnp.bitwise_and(lanes, rows - 1))
        parts.append(seen)
    return jnp.concatenate(parts, axis=0)


def forward_part(scal, first_ref, q_ref, blocks, backs, top_ref, sum_ref, acc_ref):
    allowed = allowed_keys(scal, first_ref, backs, q_ref.shape[0])
    for g in range(KVH):
        s = dot_nt(keys_of(blocks, g), heads_of(q_ref, g)) * TO_TWO
        s = jnp.where(allowed, s, neg_big)
        top = top_ref[g]
        new_top = jnp.maximum(top, jnp.max(s, axis=0, keepdims=True))
        e = jnp.exp2(s - new_top)
        shrink = jnp.exp2(top - new_top)
        top_ref[g] = new_top
        sum_ref[g] = sum_ref[g] * shrink + jnp.sum(e, axis=0, keepdims=True)
        acc_ref[g] = acc_ref[g] * shrink + dot_tn(values_of(blocks, g), e.astype(jnp.bfloat16))


def backward_part(scal, first_ref, q_ref, g_ref, blocks, backs, log_ref, inner_ref, acc_ref, outs):
    rows = q_ref.shape[0]
    allowed = allowed_keys(scal, first_ref, backs, rows)
    for g in range(KVH):
        k, v = keys_of(blocks, g), values_of(blocks, g)
        q, grads = heads_of(q_ref, g), heads_of(g_ref, g)
        s = dot_nt(k, q) * TO_TWO - log_ref[g]
        probs = jnp.exp2(jnp.where(allowed, s, neg_big))
        grad_probs = dot_nt(v, grads)
        grad_scores = (probs * (grad_probs - inner_ref[g])).astype(jnp.bfloat16)
        acc_ref[g] = acc_ref[g] + dot_tn(k, grad_scores)
        grad_k = dot_nn(grad_scores, q) * SCALE
        grad_v = dot_nn(probs.astype(jnp.bfloat16), grads)
        for i, out in enumerate(outs):
            part = slice(i * rows, (i + 1) * rows)
            out[:, g * HD : (g + 1) * HD] = grad_k[part].astype(out.dtype)
            out[:, WIDE + g * HD : WIDE + (g + 1) * HD] = grad_v[part].astype(out.dtype)


def backs_of(scal, step):
    near, far = step, 15 - step
    odd = scal[2] == 1
    return [jnp.where(odd, far, near), jnp.where(odd, near, far)]


class Near:
    def __init__(self, scal, a, b):
        self.even, self.a, self.b = scal[2] == 0, a, b

    def __getitem__(self, at):
        return jnp.where(self.even, self.a[at], self.b[at])


def pack_kernel(k_ref, v_ref, out_ref, sems):
    copies = [
        pltpu.make_async_copy(k_ref, out_ref.at[:, pl.ds(0, WIDE)], sems.at[0]),
        pltpu.make_async_copy(v_ref, out_ref.at[:, pl.ds(WIDE, WIDE)], sems.at[1]),
    ]
    for copy in copies:
        copy.start()
    for copy in copies:
        copy.wait()


def own_forward_kernel(scal, first_ref, q_ref, g_ref, own, top, total, acc, turned):
    top[...] = jnp.full(top.shape, neg_big, jnp.float32)
    total[...] = jnp.zeros(total.shape, jnp.float32)
    acc[...] = jnp.zeros(acc.shape, jnp.float32)
    forward_part(scal, first_ref, q_ref, [own], [0], top, total, acc)
    for g in range(KVH):
        turned[g] = heads_of(g_ref, g).astype(jnp.float32).T


def forward_kernel(groups, scal, first_ref, q_ref, top_in, total_in, acc_in, *rest):
    blocks, (top, total, acc) = rest[:-3], rest[-3:]
    top[...] = top_in[...]
    total[...] = total_in[...]
    acc[...] = acc_in[...]
    at = 0
    for kind, step in groups:
        count = {"near": 4, "pair": 2, "a": 1, "b": 1}[kind]
        some = blocks[at : at + count]
        at += count

        @pl.when(scal[1] >= step)
        def _(kind=kind, step=step, some=some):
            if kind == "near":
                use = [Near(scal, some[0], some[1]), Near(scal, some[2], some[3])]
                backs = [1, 2]
            else:
                use, backs = list(some), backs_of(scal, step)
                backs = {"pair": backs, "a": backs[:1], "b": backs[1:]}[kind]
            forward_part(scal, first_ref, q_ref, use, backs, top, total, acc)


def back_step(step, chosen, scal, first_ref, q_ref, g_ref, blocks, log_ref, inner_ref, acc, terms):
    @pl.when(scal[1] >= step)
    def _():
        backs = backs_of(scal, step)[chosen]
        backward_part(
            scal, first_ref, q_ref, g_ref, blocks, backs, log_ref, inner_ref, acc, terms
        )

    @pl.when(scal[1] < step)
    def _():
        for term in terms:
            term[...] = jnp.zeros(term.shape, term.dtype)


def middle_kernel(
    scal, first_ref, q_ref, g_ref, turned, top_in, total_in, acc_in, a, b,
    attended, log_ref, inner_ref, gq_acc, term_a,
):
    log_ref[...] = top_in[...]
    inner_ref[...] = total_in[...]
    attended[...] = acc_in[...]

    @pl.when(scal[1] >= STEPS)
    def _():
        backs = backs_of(scal, STEPS)[1:]
        forward_part(scal, first_ref, q_ref, [b], backs, log_ref, inner_ref, attended)

    for g in range(KVH):
        total = inner_ref[g]
        attended[g] = attended[g] * (1.0 / total)
        log_ref[g] = log_ref[g] + jnp.log2(total)
        inner_ref[g] = jnp.sum(attended[g] * turned[g], axis=0, keepdims=True)
    gq_acc[...] = jnp.zeros(gq_acc.shape, jnp.float32)
    back_step(
        STEPS, slice(0, 1), scal, first_ref, q_ref, g_ref, [a], log_ref, inner_ref, gq_acc, [term_a]
    )


def second_kernel(
    scal, first_ref, q_ref, g_ref, log_ref, inner_ref, acc_in, attended, b, acc, term_b, out_ref
):
    acc[...] = acc_in[...]
    back_step(
        STEPS, slice(1, 2), scal, first_ref, q_ref, g_ref, [b], log_ref, inner_ref, acc, [term_b]
    )
    for g in range(KVH):
        put_heads(out_ref, g, attended[g])


def back_kernel(
    step, scal, first_ref, q_ref, g_ref, log_ref, inner_ref, acc_in, a, b, acc, term_a, term_b
):
    acc[...] = acc_in[...]
    back_step(
        step, slice(0, 2), scal, first_ref, q_ref, g_ref, [a, b], log_ref, inner_ref, acc,
        [term_a, term_b],
    )


def near_back_kernel(
    scal, first_ref, q_ref, g_ref, log_ref, inner_ref, acc_in, a1, b1, a2, b2,
    acc, term_a1, term_b1, term_a2, term_b2,
):
    acc[...] = acc_in[...]
    for term in (term_a1, term_b1, term_a2, term_b2):
        term[...] = jnp.zeros(term.shape, term.dtype)

    def run(blocks, terms):
        backward_part(
            scal, first_ref, q_ref, g_ref, blocks, [1, 2], log_ref, inner_ref, acc, terms
        )

    @pl.when((scal[1] >= 1) & (scal[2] == 0))
    def _():
        run([a1, a2], [term_a1, term_a2])

    @pl.when((scal[1] >= 1) & (scal[2] == 1))
    def _():
        run([b1, b2], [term_b1, term_b2])


def own_back_kernel(
    scal, first_ref, q_ref, g_ref, log_ref, inner_ref, acc_in, own, gq_ref, term_0, acc
):
    acc[...] = acc_in[...]
    backward_part(
        scal, first_ref, q_ref, g_ref, [own], [0], log_ref, inner_ref, acc, [term_0]
    )
    for g in range(KVH):
        put_heads(gq_ref, g, acc[g] * SCALE)


ROW = jax.ShapeDtypeStruct((KVH, 1, LANES), jnp.float32)
TURNED = jax.ShapeDtypeStruct((KVH, HD, LANES), jnp.float32)


def call(kernel, outs, work, scal, *operands, scratch=()):
    in_vmem = pl.BlockSpec(memory_space=pltpu.VMEM)
    return pl.pallas_call(
        kernel,
        out_shape=outs,
        in_specs=[pl.BlockSpec(memory_space=pltpu.SMEM)] + [in_vmem] * len(operands),
        out_specs=[in_vmem] * len(outs),
        scratch_shapes=list(scratch),
        compiler_params=pltpu.CompilerParams(vmem_limit_bytes=24 * 1024 * 1024),
        cost_estimate=pl.CostEstimate(
            flops=int(work * 1.0e9), bytes_accessed=4 * 1024 * 1024, transcendentals=1 << 20
        ),
    )(scal, *operands)


def pack(keys, values):
    rows = keys.shape[0]
    return pl.pallas_call(
        pack_kernel,
        out_shape=jax.ShapeDtypeStruct((rows, 2 * WIDE), keys.dtype),
        in_specs=[pl.BlockSpec(memory_space=pltpu.HBM)] * 2,
        out_specs=pl.BlockSpec(memory_space=pltpu.VMEM),
        scratch_shapes=[pltpu.SemaphoreType.DMA((2,))],
    )(keys, values)


def both_ways(x, near_pairs, far_pairs, flip):
    windows, count = lax.axis_size("dp"), lax.axis_size("ctx")
    pairs = []
    for window in range(windows):
        chosen = near_pairs if (window + flip) % 2 == 0 else far_pairs
        pairs += [(window * count + i, window * count + j) for i, j in chosen]
    return lax.ppermute(x, ("dp", "ctx"), pairs)


def gather_pairs(step, count):
    near = [(j, j + 1) for j in range(step - 1, count - 1)]
    blocks = range(count - STEPS - 1)
    start = 0 if step == 1 else step
    far = [((b - start) % count, (b - step - 1) % count) for b in blocks]
    return near, far


def return_pairs(step, count):
    near = [(j, j - 1) for j in range(STEPS + 1 - step, count)]
    blocks = range(count - STEPS - 1)
    end = STEPS + 1 + step if step < STEPS else count
    far = [((b + STEPS + step) % count, (b + end) % count) for b in blocks]
    return near, far


def add_low(a, b):
    return (a.astype(jnp.float32) + b.astype(jnp.float32)).astype(jnp.bfloat16)


def local(queries, keys, values, out_grad, segment_ids):
    rows = queries.shape[0]
    count = lax.axis_size("ctx")
    odd = lax.rem(lax.axis_index("dp"), 2)
    q_start = lax.axis_index("ctx") * rows
    own = pack(keys, values)
    q_seg = lax.dynamic_slice_in_dim(segment_ids, q_start, rows, 0)
    first = jnp.sum((segment_ids[:, None] < q_seg[None, :]).astype(jnp.int32), axis=0, keepdims=True)
    scal = jnp.stack([q_start, (q_start - first[0, 0] + rows - 1) // rows, odd]).astype(jnp.int32)

    block = jax.ShapeDtypeStruct(own.shape, jnp.bfloat16)
    exact = jax.ShapeDtypeStruct(own.shape, jnp.float32)
    wide = jax.ShapeDtypeStruct(queries.shape, jnp.bfloat16)
    state = [ROW, ROW, TURNED]
    top, total, acc, turned = call(
        own_forward_kernel, state + [TURNED], 1.0, scal, first, queries, out_grad, own
    )

    def forward(groups, work, now, *blocks):
        kernel = functools.partial(forward_kernel, groups)
        return call(kernel, state, work, scal, first, queries, *now, *blocks)

    now = (top, total, acc)
    a, b, tops = [own], [own], {}
    for step in range(1, STEPS + 1):
        pairs = gather_pairs(step, count)
        to_a, to_b = a[-1], b[-1]
        if step == 1:
            to_b, _ = lax.optimization_barrier((to_b, top))
        if step in (5, 7):
            to_a, _ = lax.optimization_barrier((to_a, tops[step - 3]))
        a.append(both_ways(to_a, *pairs, 0))
        b.append(both_ways(to_b, *pairs, 1))
        if step == 2:
            now = forward((("near", 1),), 0.8, now, a[1], b[1], a[2], b[2])
        elif step in (4, 6):
            groups = (("pair", step - 1), ("pair", step))
            now = forward(groups, 1.0, now, a[step - 1], b[step - 1], a[step], b[step])
        tops[step] = now[0]
    now = forward((("a", STEPS),), 0.5, now, a[STEPS])
    attended_t, log_total, inner, acc, sum_a = call(
        middle_kernel, [TURNED, ROW, ROW, TURNED, block], 1.5,
        scal, first, queries, out_grad, turned, *now, a[STEPS], b[STEPS],
    )

    def backward(kernel, outs, work, *operands, scratch=()):
        return call(
            kernel, outs, work, scal, first, queries, out_grad, log_total, inner, acc, *operands,
            scratch=scratch,
        )

    acc, sum_b, attended = backward(
        second_kernel, [TURNED, block, wide], 1.0, attended_t, b[STEPS]
    )
    for step in range(1, STEPS + 1):
        pairs = return_pairs(step, count)
        sum_a = both_ways(sum_a, *pairs, 0)
        sum_b = both_ways(sum_b, *pairs, 1)
        back = STEPS - step
        if back >= 3:
            acc, term_a, term_b = backward(
                functools.partial(back_kernel, back), [TURNED, block, block], 1.2, a[back], b[back]
            )
        elif back == 2:
            acc, *terms = backward(
                near_back_kernel, [TURNED] + [block] * 4, 1.2, a[1], b[1], a[2], b[2]
            )
            term_a, term_b = terms[2:]
        elif back == 1:
            term_a, term_b = terms[:2]
            acc, _ = lax.optimization_barrier((acc, sum_a))
            grad_query, term_0 = backward(
                own_back_kernel, [wide, exact], 1.0, own, scratch=[pltpu.VMEM(TURNED.shape, jnp.float32)]
            )
        if back >= 1:
            sum_a, sum_b = add_low(sum_a, term_a), add_low(sum_b, term_b)
    summed = sum_a.astype(jnp.float32) + sum_b.astype(jnp.float32) + term_0
    return (attended, grad_query, summed[:, :WIDE], summed[:, WIDE:])


def solution(mesh):
    placed = P(("dp", "ctx"), None)
    return jax.shard_map(
        local,
        mesh=mesh,
        in_specs=(placed, placed, placed, placed, P("dp")),
        out_specs=(placed, placed, placed, placed),
        check_vma=False,
    )
```

```python
import functools
import math

import jax
import jax.numpy as jnp
from jax import lax
from jax.experimental import pallas as pl
from jax.experimental.pallas import tpu as pltpu
from jax.sharding import PartitionSpec as P

KVH = 4
HD = 128
GROUP = 4
WIDE = KVH * HD
FAR = 12
STEPS = 7
LANES = GROUP * 128
SCALE = 1.0 / math.sqrt(HD)
TO_TWO = SCALE / math.log(2.0)

neg_big = -1e30


def dot_nt(a, b):
    return lax.dot_general(a, b, (((1,), (1,)), ((), ())), preferred_element_type=jnp.float32)


def dot_nn(a, b):
    return lax.dot_general(a, b, (((1,), (0,)), ((), ())), preferred_element_type=jnp.float32)


def dot_tn(a, b):
    return lax.dot_general(a, b, (((0,), (0,)), ((), ())), preferred_element_type=jnp.float32)


def heads_of(ref, g):
    base = g * GROUP * HD
    return jnp.concatenate(
        [ref[:, base + r * HD : base + (r + 1) * HD] for r in range(GROUP)], axis=0
    )


def put_heads(ref, g, turned):
    flat = turned.T
    rows = ref.shape[0]
    for r in range(GROUP):
        cols = slice((g * GROUP + r) * HD, (g * GROUP + r + 1) * HD)
        ref[:, cols] = flat[r * rows : (r + 1) * rows].astype(ref.dtype)


def keys_of(blocks, g):
    return jnp.concatenate([b[:, g * HD : (g + 1) * HD] for b in blocks], axis=0)


def values_of(blocks, g):
    return jnp.concatenate([b[:, WIDE + g * HD : WIDE + (g + 1) * HD] for b in blocks], axis=0)


def allowed_keys(scal, first_ref, backs, rows):
    q_start = scal[0]
    first = jnp.concatenate([first_ref[...]] * GROUP, axis=1)
    within = lax.broadcasted_iota(jnp.int32, (rows, LANES), 0)
    parts = []
    for back in backs:
        place = (q_start - back * rows) + within
        seen = place >= first
        if isinstance(back, int) and back == 0:
            lanes = lax.broadcasted_iota(jnp.int32, (rows, LANES), 1)
            seen = seen & (within <= jnp.bitwise_and(lanes, rows - 1))
        parts.append(seen)
    return jnp.concatenate(parts, axis=0)


def forward_part(scal, first_ref, q_ref, g_ref, blocks, backs, top_ref, sum_ref, acc_ref, e_ref, gp_ref):
    allowed = allowed_keys(scal, first_ref, backs, q_ref.shape[0])
    for g in range(KVH):
        v = values_of(blocks, g)
        s = dot_nt(keys_of(blocks, g), heads_of(q_ref, g)) * TO_TWO
        s = jnp.where(allowed, s, neg_big)
        top = top_ref[g]
        new_top = jnp.maximum(top, jnp.max(s, axis=0, keepdims=True))
        e = jnp.exp2(s - new_top)
        shrink = jnp.exp2(top - new_top)
        e_low = e.astype(jnp.bfloat16)
        e_ref[g] = e_low
        gp_ref[g] = dot_nt(v, heads_of(g_ref, g)).astype(jnp.bfloat16)
        top_ref[g] = new_top
        sum_ref[g] = sum_ref[g] * shrink + jnp.sum(e, axis=0, keepdims=True)
        acc_ref[g] = acc_ref[g] * shrink + dot_tn(v, e_low)


def backward_part(q_ref, g_ref, blocks, factors, inner_ref, acc_ref, e_ref, gp_ref, outs):
    rows = q_ref.shape[0]
    for g in range(KVH):
        probs = e_ref[g].astype(jnp.float32) * factors[g]
        grad_scores = (probs * (gp_ref[g].astype(jnp.float32) - inner_ref[g])).astype(jnp.bfloat16)
        acc_ref[g] = acc_ref[g] + dot_tn(keys_of(blocks, g), grad_scores)
        grad_k = dot_nn(grad_scores, heads_of(q_ref, g)) * SCALE
        grad_v = dot_nn(probs.astype(jnp.bfloat16), heads_of(g_ref, g))
        for i, out in enumerate(outs):
            part = slice(i * rows, (i + 1) * rows)
            out[:, g * HD : (g + 1) * HD] = grad_k[part].astype(out.dtype)
            out[:, WIDE + g * HD : WIDE + (g + 1) * HD] = grad_v[part].astype(out.dtype)


def factors_of(top_ref, log_ref):
    return [jnp.exp2(top_ref[g] - log_ref[g]) for g in range(KVH)]


def clear(terms):
    for term in terms:
        term[...] = jnp.zeros(term.shape, term.dtype)


def backs_of(scal, step):
    near, far = step, 15 - step
    odd = scal[2] == 1
    return [jnp.where(odd, far, near), jnp.where(odd, near, far)]


class Near:
    def __init__(self, scal, a, b):
        self.even, self.a, self.b = scal[2] == 0, a, b

    def __getitem__(self, at):
        return jnp.where(self.even, self.a[at], self.b[at])


def pack_kernel(k_ref, v_ref, out_ref, sems):
    copies = [
        pltpu.make_async_copy(k_ref, out_ref.at[:, pl.ds(0, WIDE)], sems.at[0]),
        pltpu.make_async_copy(v_ref, out_ref.at[:, pl.ds(WIDE, WIDE)], sems.at[1]),
    ]
    for copy in copies:
        copy.start()
    for copy in copies:
        copy.wait()


def own_forward_kernel(scal, first_ref, q_ref, g_ref, own, top, total, acc, e, gp, turned):
    top[...] = jnp.full(top.shape, neg_big, jnp.float32)
    total[...] = jnp.zeros(total.shape, jnp.float32)
    acc[...] = jnp.zeros(acc.shape, jnp.float32)
    forward_part(scal, first_ref, q_ref, g_ref, [own], [0], top, total, acc, e, gp)
    for g in range(KVH):
        turned[g] = heads_of(g_ref, g).astype(jnp.float32).T


def forward_kernel(kind, step, scal, first_ref, q_ref, g_ref, top_in, total_in, acc_in, *rest):
    blocks, (top, total, acc, e, gp) = rest[:-5], rest[-5:]
    top[...] = top_in[...]
    total[...] = total_in[...]
    acc[...] = acc_in[...]

    @pl.when(scal[1] >= step)
    def _():
        if kind == "near":
            a1, b1, a2, b2 = blocks
            use, backs = [Near(scal, a1, b1), Near(scal, a2, b2)], [1, 2]
        else:
            use, backs = list(blocks), backs_of(scal, step)[: len(blocks)]
        forward_part(scal, first_ref, q_ref, g_ref, use, backs, top, total, acc, e, gp)


def middle_kernel(
    scal, first_ref, q_ref, g_ref, turned, top_in, total_in, acc_in, e_a, gp_a, a, b,
    attended, log_ref, inner_ref, gq_acc, term_a, term_b, e_b, gp_b,
):
    log_ref[...] = top_in[...]
    inner_ref[...] = total_in[...]
    attended[...] = acc_in[...]
    gq_acc[...] = jnp.zeros(gq_acc.shape, jnp.float32)

    @pl.when(scal[1] >= STEPS)
    def _():
        backs = backs_of(scal, STEPS)[1:]
        forward_part(
            scal, first_ref, q_ref, g_ref, [b], backs, log_ref, inner_ref, attended, e_b, gp_b
        )

    inverse = []
    for g in range(KVH):
        total = inner_ref[g]
        inverse.append(1.0 / total)
        attended[g] = attended[g] * inverse[g]
        log_ref[g] = log_ref[g] + jnp.log2(total)
        inner_ref[g] = jnp.sum(attended[g] * turned[g], axis=0, keepdims=True)

    @pl.when(scal[1] >= STEPS)
    def _():
        backward_part(
            q_ref, g_ref, [a], factors_of(top_in, log_ref), inner_ref, gq_acc, e_a, gp_a, [term_a]
        )
        backward_part(q_ref, g_ref, [b], inverse, inner_ref, gq_acc, e_b, gp_b, [term_b])

    @pl.when(scal[1] < STEPS)
    def _():
        clear([term_a, term_b])


def pair_back(step, scal, q_ref, g_ref, log_ref, inner_ref, top, e, gp, a, b, acc, term_a, term_b):
    @pl.when(scal[1] >= step)
    def _():
        backward_part(
            q_ref, g_ref, [a, b], factors_of(top, log_ref), inner_ref, acc, e, gp, [term_a, term_b]
        )

    @pl.when(scal[1] < step)
    def _():
        clear([term_a, term_b])


def back_kernel(
    step, scal, q_ref, g_ref, log_ref, inner_ref, acc_in, top, e, gp, a, b, acc, term_a, term_b
):
    acc[...] = acc_in[...]
    pair_back(step, scal, q_ref, g_ref, log_ref, inner_ref, top, e, gp, a, b, acc, term_a, term_b)


def second_kernel(
    step, scal, q_ref, g_ref, log_ref, inner_ref, acc_in, top, e, gp, a, b, attended,
    acc, term_a, term_b, out_ref,
):
    acc[...] = acc_in[...]
    pair_back(step, scal, q_ref, g_ref, log_ref, inner_ref, top, e, gp, a, b, acc, term_a, term_b)
    for g in range(KVH):
        put_heads(out_ref, g, attended[g])


def near_back_kernel(
    scal, q_ref, g_ref, log_ref, inner_ref, acc_in, top, e, gp, a1, b1, a2, b2,
    acc, term_a1, term_b1, term_a2, term_b2,
):
    acc[...] = acc_in[...]
    clear([term_a1, term_b1, term_a2, term_b2])

    def run(blocks, terms):
        backward_part(
            q_ref, g_ref, blocks, factors_of(top, log_ref), inner_ref, acc, e, gp, terms
        )

    @pl.when((scal[1] >= 1) & (scal[2] == 0))
    def _():
        run([a1, a2], [term_a1, term_a2])

    @pl.when((scal[1] >= 1) & (scal[2] == 1))
    def _():
        run([b1, b2], [term_b1, term_b2])


def own_back_kernel(
    scal, q_ref, g_ref, log_ref, inner_ref, acc_in, top, e, gp, own, gq_ref, term_0, acc
):
    acc[...] = acc_in[...]
    backward_part(
        q_ref, g_ref, [own], factors_of(top, log_ref), inner_ref, acc, e, gp, [term_0]
    )
    for g in range(KVH):
        put_heads(gq_ref, g, acc[g] * SCALE)


ROW = jax.ShapeDtypeStruct((KVH, 1, LANES), jnp.float32)
TURNED = jax.ShapeDtypeStruct((KVH, HD, LANES), jnp.float32)


def call(kernel, outs, work, scal, *operands, scratch=()):
    in_vmem = pl.BlockSpec(memory_space=pltpu.VMEM)
    return pl.pallas_call(
        kernel,
        out_shape=outs,
        in_specs=[pl.BlockSpec(memory_space=pltpu.SMEM)] + [in_vmem] * len(operands),
        out_specs=[in_vmem] * len(outs),
        scratch_shapes=list(scratch),
        compiler_params=pltpu.CompilerParams(vmem_limit_bytes=24 * 1024 * 1024),
        cost_estimate=pl.CostEstimate(
            flops=int(work * 1.0e9), bytes_accessed=4 * 1024 * 1024, transcendentals=1 << 20
        ),
    )(scal, *operands)


def pack(keys, values):
    rows = keys.shape[0]
    return pl.pallas_call(
        pack_kernel,
        out_shape=jax.ShapeDtypeStruct((rows, 2 * WIDE), keys.dtype),
        in_specs=[pl.BlockSpec(memory_space=pltpu.HBM)] * 2,
        out_specs=pl.BlockSpec(memory_space=pltpu.VMEM),
        scratch_shapes=[pltpu.SemaphoreType.DMA((2,))],
    )(keys, values)


def both_ways(x, near_pairs, far_pairs, flip):
    windows, count = lax.axis_size("dp"), lax.axis_size("ctx")
    pairs = []
    for window in range(windows):
        chosen = near_pairs if (window + flip) % 2 == 0 else far_pairs
        pairs += [(window * count + i, window * count + j) for i, j in chosen]
    return lax.ppermute(x, ("dp", "ctx"), pairs)


def gather_pairs(step, count):
    near = [(j, j + 1) for j in range(step - 1, count - 1)]
    blocks = range(count - STEPS - 1)
    start = 0 if step == 1 else step
    far = [((b - start) % count, (b - step - 1) % count) for b in blocks]
    return near, far


def return_pairs(step, count):
    near = [(j, j - 1) for j in range(STEPS + 1 - step, count)]
    blocks = range(count - STEPS - 1)
    end = STEPS + 1 + step if step < STEPS else count
    far = [((b + STEPS + step) % count, (b + end) % count) for b in blocks]
    return near, far


def add_low(a, b):
    return (a.astype(jnp.float32) + b.astype(jnp.float32)).astype(jnp.bfloat16)


def local(queries, keys, values, out_grad, segment_ids):
    rows = queries.shape[0]
    count = lax.axis_size("ctx")
    odd = lax.rem(lax.axis_index("dp"), 2)
    q_start = lax.axis_index("ctx") * rows
    own = pack(keys, values)
    q_seg = lax.dynamic_slice_in_dim(segment_ids, q_start, rows, 0)
    first = jnp.sum((segment_ids[:, None] < q_seg[None, :]).astype(jnp.int32), axis=0, keepdims=True)
    scal = jnp.stack([q_start, (q_start - first[0, 0] + rows - 1) // rows, odd]).astype(jnp.int32)

    block = jax.ShapeDtypeStruct(own.shape, jnp.bfloat16)
    exact = jax.ShapeDtypeStruct(own.shape, jnp.float32)
    wide = jax.ShapeDtypeStruct(queries.shape, jnp.bfloat16)
    state = [ROW, ROW, TURNED]
    one = [jax.ShapeDtypeStruct((KVH, rows, LANES), jnp.bfloat16)] * 2
    two = [jax.ShapeDtypeStruct((KVH, 2 * rows, LANES), jnp.bfloat16)] * 2
    *now, e, gp, turned = call(
        own_forward_kernel, state + one + [TURNED], 1.0, scal, first, queries, out_grad, own
    )
    kept = {0: (now[0], e, gp)}

    def forward(kind, step, *blocks):
        *state_now, e, gp = call(
            functools.partial(forward_kernel, kind, step), state + (one if kind == "a" else two), 1.0,
            scal, first, queries, out_grad, *now, *blocks,
        )
        kept[step] = (state_now[0], e, gp)
        return state_now

    a, b, tops = [own], [own], {1: now[0]}
    for step in range(1, STEPS + 1):
        pairs = gather_pairs(step, count)
        to_a = a[-1]
        if step >= 3:
            to_a, _ = lax.optimization_barrier((to_a, tops[step - 2]))
        a.append(both_ways(to_a, *pairs, 0))
        b.append(both_ways(b[-1], *pairs, 1))
        if step == 2:
            now = forward("near", 1, a[1], b[1], a[2], b[2])
        elif 3 <= step < STEPS:
            now = forward("pair", step, a[step], b[step])
        tops[step] = now[0]
    now = forward("a", STEPS, a[STEPS])
    part = pltpu.VMEM(one[0].shape, jnp.bfloat16)
    attended_t, log_total, inner, acc, sum_a, sum_b = call(
        middle_kernel, [TURNED, ROW, ROW, TURNED, block, block], 1.5,
        scal, first, queries, out_grad, turned, *now, *kept[STEPS][1:], a[STEPS], b[STEPS],
        scratch=[part, part],
    )

    def backward(kernel, outs, step, *operands, scratch=()):
        return call(
            kernel, outs, 1.0, scal, queries, out_grad, log_total, inner, acc, *kept[step], *operands,
            scratch=scratch,
        )

    for step in range(1, STEPS + 1):
        pairs = return_pairs(step, count)
        sum_a = both_ways(sum_a, *pairs, 0)
        sum_b = both_ways(sum_b, *pairs, 1)
        back = STEPS - step
        if back == 6:
            acc, term_a, term_b, attended = backward(
                functools.partial(second_kernel, back), [TURNED, block, block, wide], back,
                a[back], b[back], attended_t,
            )
        elif back >= 3:
            acc, term_a, term_b = backward(
                functools.partial(back_kernel, back), [TURNED, block, block], back, a[back], b[back]
            )
        elif back == 2:
            acc, *terms = backward(
                near_back_kernel, [TURNED] + [block] * 4, 1, a[1], b[1], a[2], b[2]
            )
            term_a, term_b = terms[2:]
        elif back == 1:
            term_a, term_b = terms[:2]
            acc, _ = lax.optimization_barrier((acc, sum_a))
            grad_query, term_0 = backward(
                own_back_kernel, [wide, exact], 0, own, scratch=[pltpu.VMEM(TURNED.shape, jnp.float32)]
            )
        if back >= 1:
            sum_a, sum_b = add_low(sum_a, term_a), add_low(sum_b, term_b)
    summed = sum_a.astype(jnp.float32) + sum_b.astype(jnp.float32) + term_0
    return (attended, grad_query, summed[:, :WIDE], summed[:, WIDE:])


def solution(mesh):
    placed = P(("dp", "ctx"), None)
    return jax.shard_map(
        local,
        mesh=mesh,
        in_specs=(placed, placed, placed, placed, P("dp")),
        out_specs=(placed, placed, placed, placed),
        check_vma=False,
    )
```

```python
import functools
import math

import jax
import jax.numpy as jnp
from jax import lax
from jax.experimental import pallas as pl
from jax.experimental.pallas import tpu as pltpu
from jax.sharding import PartitionSpec as P

KVH = 4
HD = 128
GROUP = 4
WIDE = KVH * HD
FAR = 12
STEPS = 7
LANES = GROUP * 128
SCALE = 1.0 / math.sqrt(HD)
TO_TWO = SCALE / math.log(2.0)

neg_big = -1e30


def dot_nt(a, b):
    return lax.dot_general(a, b, (((1,), (1,)), ((), ())), preferred_element_type=jnp.float32)


def dot_nn(a, b):
    return lax.dot_general(a, b, (((1,), (0,)), ((), ())), preferred_element_type=jnp.float32)


def dot_tn(a, b):
    return lax.dot_general(a, b, (((0,), (0,)), ((), ())), preferred_element_type=jnp.float32)


def heads_of(ref, g):
    base = g * GROUP * HD
    return jnp.concatenate(
        [ref[:, base + r * HD : base + (r + 1) * HD] for r in range(GROUP)], axis=0
    )


def put_heads(ref, g, turned):
    flat = turned.T
    rows = ref.shape[0]
    for r in range(GROUP):
        cols = slice((g * GROUP + r) * HD, (g * GROUP + r + 1) * HD)
        ref[:, cols] = flat[r * rows : (r + 1) * rows].astype(ref.dtype)


def keys_of(blocks, g):
    return jnp.concatenate([b[:, g * HD : (g + 1) * HD] for b in blocks], axis=0)


def values_of(blocks, g):
    return jnp.concatenate([b[:, WIDE + g * HD : WIDE + (g + 1) * HD] for b in blocks], axis=0)


def allowed_keys(scal, first_ref, backs, rows):
    q_start = scal[0]
    first = jnp.concatenate([first_ref[...]] * GROUP, axis=1)
    within = lax.broadcasted_iota(jnp.int32, (rows, LANES), 0)
    parts = []
    for back in backs:
        place = (q_start - back * rows) + within
        seen = place >= first
        if isinstance(back, int) and back == 0:
            lanes = lax.broadcasted_iota(jnp.int32, (rows, LANES), 1)
            seen = seen & (within <= jnp.bitwise_and(lanes, rows - 1))
        parts.append(seen)
    return jnp.concatenate(parts, axis=0)


def forward_part(scal, first_ref, q_ref, g_ref, blocks, backs, top_ref, sum_ref, acc_ref, e_ref, gp_ref):
    allowed = allowed_keys(scal, first_ref, backs, q_ref.shape[0])
    for g in range(KVH):
        v = values_of(blocks, g)
        s = dot_nt(keys_of(blocks, g), heads_of(q_ref, g)) * TO_TWO
        s = jnp.where(allowed, s, neg_big)
        top = top_ref[g]
        new_top = jnp.maximum(top, jnp.max(s, axis=0, keepdims=True))
        e = jnp.exp2(s - new_top)
        shrink = jnp.exp2(top - new_top)
        e_low = e.astype(jnp.bfloat16)
        e_ref[g] = e_low
        gp_ref[g] = dot_nt(v, heads_of(g_ref, g)).astype(jnp.bfloat16)
        top_ref[g] = new_top
        sum_ref[g] = sum_ref[g] * shrink + jnp.sum(e, axis=0, keepdims=True)
        acc_ref[g] = acc_ref[g] * shrink + dot_tn(v, e_low)


def backward_part(q_ref, g_ref, blocks, factors, inner_ref, acc_ref, e_ref, gp_ref, outs):
    rows = q_ref.shape[0]
    for g in range(KVH):
        probs = e_ref[g].astype(jnp.float32) * factors[g]
        grad_scores = (probs * (gp_ref[g].astype(jnp.float32) - inner_ref[g])).astype(jnp.bfloat16)
        acc_ref[g] = acc_ref[g] + dot_tn(keys_of(blocks, g), grad_scores)
        grad_k = dot_nn(grad_scores, heads_of(q_ref, g)) * SCALE
        grad_v = dot_nn(probs.astype(jnp.bfloat16), heads_of(g_ref, g))
        for i, out in enumerate(outs):
            part = slice(i * rows, (i + 1) * rows)
            out[:, g * HD : (g + 1) * HD] = grad_k[part].astype(out.dtype)
            out[:, WIDE + g * HD : WIDE + (g + 1) * HD] = grad_v[part].astype(out.dtype)


def factors_of(top_ref, log_ref):
    return [jnp.exp2(top_ref[g] - log_ref[g]) for g in range(KVH)]


def clear(terms):
    for term in terms:
        term[...] = jnp.zeros(term.shape, term.dtype)


def backs_of(scal, step):
    near, far = step, 15 - step
    odd = scal[2] == 1
    return [jnp.where(odd, far, near), jnp.where(odd, near, far)]


class Near:
    def __init__(self, scal, a, b):
        self.even, self.a, self.b = scal[2] == 0, a, b

    def __getitem__(self, at):
        return jnp.where(self.even, self.a[at], self.b[at])


def pack_kernel(k_ref, v_ref, out_ref, sems):
    copies = [
        pltpu.make_async_copy(k_ref, out_ref.at[:, pl.ds(0, WIDE)], sems.at[0]),
        pltpu.make_async_copy(v_ref, out_ref.at[:, pl.ds(WIDE, WIDE)], sems.at[1]),
    ]
    for copy in copies:
        copy.start()
    for copy in copies:
        copy.wait()


def own_forward_kernel(scal, first_ref, q_ref, g_ref, own, top, total, acc, e, gp, turned):
    top[...] = jnp.full(top.shape, neg_big, jnp.float32)
    total[...] = jnp.zeros(total.shape, jnp.float32)
    acc[...] = jnp.zeros(acc.shape, jnp.float32)
    forward_part(scal, first_ref, q_ref, g_ref, [own], [0], top, total, acc, e, gp)
    for g in range(KVH):
        turned[g] = heads_of(g_ref, g).astype(jnp.float32).T


def forward_kernel(kind, step, scal, first_ref, q_ref, g_ref, top_in, total_in, acc_in, *rest):
    blocks, (top, total, acc, e, gp) = rest[:-5], rest[-5:]
    top[...] = top_in[...]
    total[...] = total_in[...]
    acc[...] = acc_in[...]

    @pl.when(scal[1] >= step)
    def _():
        if kind == "near":
            a1, b1, a2, b2 = blocks
            use, backs = [Near(scal, a1, b1), Near(scal, a2, b2)], [1, 2]
        else:
            use, backs = list(blocks), backs_of(scal, step)[: len(blocks)]
        forward_part(scal, first_ref, q_ref, g_ref, use, backs, top, total, acc, e, gp)


def middle_kernel(
    scal, first_ref, q_ref, g_ref, turned, top_in, total_in, acc_in, e_a, gp_a, a, b,
    attended, log_ref, inner_ref, gq_acc, term_a, term_b, e_b, gp_b,
):
    log_ref[...] = top_in[...]
    inner_ref[...] = total_in[...]
    attended[...] = acc_in[...]
    gq_acc[...] = jnp.zeros(gq_acc.shape, jnp.float32)

    @pl.when(scal[1] >= STEPS)
    def _():
        backs = backs_of(scal, STEPS)[1:]
        forward_part(
            scal, first_ref, q_ref, g_ref, [b], backs, log_ref, inner_ref, attended, e_b, gp_b
        )

    inverse = []
    for g in range(KVH):
        total = inner_ref[g]
        inverse.append(1.0 / total)
        attended[g] = attended[g] * inverse[g]
        log_ref[g] = log_ref[g] + jnp.log2(total)
        inner_ref[g] = jnp.sum(attended[g] * turned[g], axis=0, keepdims=True)

    @pl.when(scal[1] >= STEPS)
    def _():
        backward_part(
            q_ref, g_ref, [a], factors_of(top_in, log_ref), inner_ref, gq_acc, e_a, gp_a, [term_a]
        )
        backward_part(q_ref, g_ref, [b], inverse, inner_ref, gq_acc, e_b, gp_b, [term_b])

    @pl.when(scal[1] < STEPS)
    def _():
        clear([term_a, term_b])


def pair_back(step, scal, q_ref, g_ref, log_ref, inner_ref, top, e, gp, a, b, acc, term_a, term_b):
    @pl.when(scal[1] >= step)
    def _():
        backward_part(
            q_ref, g_ref, [a, b], factors_of(top, log_ref), inner_ref, acc, e, gp, [term_a, term_b]
        )

    @pl.when(scal[1] < step)
    def _():
        clear([term_a, term_b])


def back_kernel(
    step, scal, q_ref, g_ref, log_ref, inner_ref, acc_in, top, e, gp, a, b, acc, term_a, term_b
):
    acc[...] = acc_in[...]
    pair_back(step, scal, q_ref, g_ref, log_ref, inner_ref, top, e, gp, a, b, acc, term_a, term_b)


def second_kernel(
    step, scal, q_ref, g_ref, log_ref, inner_ref, acc_in, top, e, gp, a, b, attended,
    acc, term_a, term_b, out_ref,
):
    acc[...] = acc_in[...]
    pair_back(step, scal, q_ref, g_ref, log_ref, inner_ref, top, e, gp, a, b, acc, term_a, term_b)
    for g in range(KVH):
        put_heads(out_ref, g, attended[g])


def near_back_kernel(
    scal, q_ref, g_ref, log_ref, inner_ref, acc_in, top, e, gp, a1, b1, a2, b2,
    acc, term_a1, term_b1, term_a2, term_b2,
):
    acc[...] = acc_in[...]
    clear([term_a1, term_b1, term_a2, term_b2])

    def run(blocks, terms):
        backward_part(
            q_ref, g_ref, blocks, factors_of(top, log_ref), inner_ref, acc, e, gp, terms
        )

    @pl.when((scal[1] >= 1) & (scal[2] == 0))
    def _():
        run([a1, a2], [term_a1, term_a2])

    @pl.when((scal[1] >= 1) & (scal[2] == 1))
    def _():
        run([b1, b2], [term_b1, term_b2])


def own_back_kernel(
    scal, q_ref, g_ref, log_ref, inner_ref, acc_in, top, e, gp, own, gq_ref, term_0, acc
):
    acc[...] = acc_in[...]
    backward_part(
        q_ref, g_ref, [own], factors_of(top, log_ref), inner_ref, acc, e, gp, [term_0]
    )
    for g in range(KVH):
        put_heads(gq_ref, g, acc[g] * SCALE)


ROW = jax.ShapeDtypeStruct((KVH, 1, LANES), jnp.float32)
TURNED = jax.ShapeDtypeStruct((KVH, HD, LANES), jnp.float32)


def call(kernel, outs, work, scal, *operands, scratch=()):
    in_vmem = pl.BlockSpec(memory_space=pltpu.VMEM)
    return pl.pallas_call(
        kernel,
        out_shape=outs,
        in_specs=[pl.BlockSpec(memory_space=pltpu.SMEM)] + [in_vmem] * len(operands),
        out_specs=[in_vmem] * len(outs),
        scratch_shapes=list(scratch),
        compiler_params=pltpu.CompilerParams(vmem_limit_bytes=24 * 1024 * 1024),
        cost_estimate=pl.CostEstimate(
            flops=int(work * 1.0e9), bytes_accessed=4 * 1024 * 1024, transcendentals=1 << 20
        ),
    )(scal, *operands)


def pack(keys, values):
    rows = keys.shape[0]
    return pl.pallas_call(
        pack_kernel,
        out_shape=jax.ShapeDtypeStruct((rows, 2 * WIDE), keys.dtype),
        in_specs=[pl.BlockSpec(memory_space=pltpu.HBM)] * 2,
        out_specs=pl.BlockSpec(memory_space=pltpu.VMEM),
        scratch_shapes=[pltpu.SemaphoreType.DMA((2,))],
    )(keys, values)


def both_ways(x, near_pairs, far_pairs, flip):
    windows, count = lax.axis_size("dp"), lax.axis_size("ctx")
    pairs = []
    for window in range(windows):
        chosen = near_pairs if flip else far_pairs
        pairs += [(window * count + i, window * count + j) for i, j in chosen]
    return lax.ppermute(x, ("dp", "ctx"), pairs)


def gather_pairs(step, count):
    near = [(j, j + 1) for j in range(step - 1, count - 1)]
    blocks = range(count - STEPS - 1)
    start = 0 if step == 1 else step
    far = [((b - start) % count, (b - step - 1) % count) for b in blocks]
    return near, far


def return_pairs(step, count):
    near = [(j, j - 1) for j in range(STEPS + 1 - step, count)]
    blocks = range(count - STEPS - 1)
    end = STEPS + 1 + step if step < STEPS else count
    far = [((b + STEPS + step) % count, (b + end) % count) for b in blocks]
    return near, far


def add_low(a, b):
    return (a.astype(jnp.float32) + b.astype(jnp.float32)).astype(jnp.bfloat16)


def local(queries, keys, values, out_grad, segment_ids):
    rows = queries.shape[0]
    count = lax.axis_size("ctx")
    odd = jnp.ones((), jnp.int32)
    q_start = lax.axis_index("ctx") * rows
    own = pack(keys, values)
    q_seg = lax.dynamic_slice_in_dim(segment_ids, q_start, rows, 0)
    first = jnp.sum((segment_ids[:, None] < q_seg[None, :]).astype(jnp.int32), axis=0, keepdims=True)
    scal = jnp.stack([q_start, (q_start - first[0, 0] + rows - 1) // rows, odd]).astype(jnp.int32)

    block = jax.ShapeDtypeStruct(own.shape, jnp.bfloat16)
    exact = jax.ShapeDtypeStruct(own.shape, jnp.float32)
    wide = jax.ShapeDtypeStruct(queries.shape, jnp.bfloat16)
    state = [ROW, ROW, TURNED]
    one = [jax.ShapeDtypeStruct((KVH, rows, LANES), jnp.bfloat16)] * 2
    two = [jax.ShapeDtypeStruct((KVH, 2 * rows, LANES), jnp.bfloat16)] * 2
    *now, e, gp, turned = call(
        own_forward_kernel, state + one + [TURNED], 1.0, scal, first, queries, out_grad, own
    )
    kept = {0: (now[0], e, gp)}

    def forward(kind, step, *blocks):
        *state_now, e, gp = call(
            functools.partial(forward_kernel, kind, step), state + (one if kind == "a" else two), 1.0,
            scal, first, queries, out_grad, *now, *blocks,
        )
        kept[step] = (state_now[0], e, gp)
        return state_now

    a, b, tops = [own], [own], {1: now[0]}
    for step in range(1, STEPS + 1):
        pairs = gather_pairs(step, count)
        to_a = a[-1]
        if step >= 3:
            to_a, _ = lax.optimization_barrier((to_a, tops[step - 2]))
        a.append(both_ways(to_a, *pairs, 0))
        b.append(both_ways(b[-1], *pairs, 1))
        if step == 2:
            now = forward("near", 1, a[1], b[1], a[2], b[2])
        elif 3 <= step < STEPS:
            now = forward("pair", step, a[step], b[step])
        tops[step] = now[0]
    now = forward("a", STEPS, a[STEPS])
    part = pltpu.VMEM(one[0].shape, jnp.bfloat16)
    attended_t, log_total, inner, acc, sum_a, sum_b = call(
        middle_kernel, [TURNED, ROW, ROW, TURNED, block, block], 1.5,
        scal, first, queries, out_grad, turned, *now, *kept[STEPS][1:], a[STEPS], b[STEPS],
        scratch=[part, part],
    )

    def backward(kernel, outs, step, *operands, scratch=()):
        return call(
            kernel, outs, 1.0, scal, queries, out_grad, log_total, inner, acc, *kept[step], *operands,
            scratch=scratch,
        )

    for step in range(1, STEPS + 1):
        pairs = return_pairs(step, count)
        sum_a = both_ways(sum_a, *pairs, 0)
        sum_b = both_ways(sum_b, *pairs, 1)
        back = STEPS - step
        if back == 6:
            acc, term_a, term_b, attended = backward(
                functools.partial(second_kernel, back), [TURNED, block, block, wide], back,
                a[back], b[back], attended_t,
            )
        elif back >= 3:
            acc, term_a, term_b = backward(
                functools.partial(back_kernel, back), [TURNED, block, block], back, a[back], b[back]
            )
        elif back == 2:
            acc, *terms = backward(
                near_back_kernel, [TURNED] + [block] * 4, 1, a[1], b[1], a[2], b[2]
            )
            term_a, term_b = terms[2:]
        elif back == 1:
            term_a, term_b = terms[:2]
            acc, _ = lax.optimization_barrier((acc, sum_a))
            grad_query, term_0 = backward(
                own_back_kernel, [wide, exact], 0, own, scratch=[pltpu.VMEM(TURNED.shape, jnp.float32)]
            )
        if back >= 1:
            sum_a, sum_b = add_low(sum_a, term_a), add_low(sum_b, term_b)
    summed = sum_a.astype(jnp.float32) + sum_b.astype(jnp.float32) + term_0
    return (attended, grad_query, summed[:, :WIDE], summed[:, WIDE:])


def solution(mesh):
    placed = P(("dp", "ctx"), None)
    return jax.shard_map(
        local,
        mesh=mesh,
        in_specs=(placed, placed, placed, placed, P("dp")),
        out_specs=(placed, placed, placed, placed),
        check_vma=False,
    )
```

```python
import functools
import math

import jax
import jax.numpy as jnp
from jax import lax
from jax.experimental import pallas as pl
from jax.experimental.pallas import tpu as pltpu
from jax.sharding import PartitionSpec as P

KVH = 4
HD = 128
GROUP = 4
WIDE = KVH * HD
FAR = 12
STEPS = 7
LANES = GROUP * 128
SCALE = 1.0 / math.sqrt(HD)
TO_TWO = SCALE / math.log(2.0)

neg_big = -1e30


def dot_nt(a, b):
    return lax.dot_general(a, b, (((1,), (1,)), ((), ())), preferred_element_type=jnp.float32)


def dot_nn(a, b):
    return lax.dot_general(a, b, (((1,), (0,)), ((), ())), preferred_element_type=jnp.float32)


def dot_tn(a, b):
    return lax.dot_general(a, b, (((0,), (0,)), ((), ())), preferred_element_type=jnp.float32)


def heads_of(ref, g):
    base = g * GROUP * HD
    return jnp.concatenate(
        [ref[:, base + r * HD : base + (r + 1) * HD] for r in range(GROUP)], axis=0
    )


def put_heads(ref, g, turned):
    flat = turned.T
    rows = ref.shape[0]
    for r in range(GROUP):
        cols = slice((g * GROUP + r) * HD, (g * GROUP + r + 1) * HD)
        ref[:, cols] = flat[r * rows : (r + 1) * rows].astype(ref.dtype)


def keys_of(blocks, g):
    return jnp.concatenate([b[:, g * HD : (g + 1) * HD] for b in blocks], axis=0)


def values_of(blocks, g):
    return jnp.concatenate([b[:, WIDE + g * HD : WIDE + (g + 1) * HD] for b in blocks], axis=0)


def allowed_keys(scal, first_ref, backs, rows):
    q_start = scal[0]
    first = jnp.concatenate([first_ref[...]] * GROUP, axis=1)
    within = lax.broadcasted_iota(jnp.int32, (rows, LANES), 0)
    parts = []
    for back in backs:
        place = (q_start - back * rows) + within
        seen = place >= first
        if isinstance(back, int) and back == 0:
            lanes = lax.broadcasted_iota(jnp.int32, (rows, LANES), 1)
            seen = seen & (within <= jnp.bitwise_and(lanes, rows - 1))
        parts.append(seen)
    return jnp.concatenate(parts, axis=0)


def forward_part(scal, first_ref, q_ref, g_ref, blocks, backs, top_ref, sum_ref, acc_ref, e_ref, gp_ref):
    allowed = allowed_keys(scal, first_ref, backs, q_ref.shape[0])
    for g in range(KVH):
        v = values_of(blocks, g)
        s = dot_nt(keys_of(blocks, g), heads_of(q_ref, g)) * TO_TWO
        s = jnp.where(allowed, s, neg_big)
        top = top_ref[g]
        new_top = jnp.maximum(top, jnp.max(s, axis=0, keepdims=True))
        e = jnp.exp2(s - new_top)
        shrink = jnp.exp2(top - new_top)
        e_low = e.astype(jnp.bfloat16)
        e_ref[g] = e_low
        gp_ref[g] = dot_nt(v, heads_of(g_ref, g)).astype(jnp.bfloat16)
        top_ref[g] = new_top
        sum_ref[g] = sum_ref[g] * shrink + jnp.sum(e, axis=0, keepdims=True)
        acc_ref[g] = acc_ref[g] * shrink + dot_tn(v, e_low)


def backward_part(q_ref, g_ref, blocks, factors, inner_ref, acc_ref, e_ref, gp_ref, outs):
    rows = q_ref.shape[0]
    for g in range(KVH):
        probs = e_ref[g].astype(jnp.float32) * factors[g]
        grad_scores = (probs * (gp_ref[g].astype(jnp.float32) - inner_ref[g])).astype(jnp.bfloat16)
        acc_ref[g] = acc_ref[g] + dot_tn(keys_of(blocks, g), grad_scores)
        grad_k = dot_nn(grad_scores, heads_of(q_ref, g)) * SCALE
        grad_v = dot_nn(probs.astype(jnp.bfloat16), heads_of(g_ref, g))
        for i, out in enumerate(outs):
            part = slice(i * rows, (i + 1) * rows)
            out[:, g * HD : (g + 1) * HD] = grad_k[part].astype(out.dtype)
            out[:, WIDE + g * HD : WIDE + (g + 1) * HD] = grad_v[part].astype(out.dtype)


def factors_of(top_ref, log_ref):
    return [jnp.exp2(top_ref[g] - log_ref[g]) for g in range(KVH)]


def clear(terms):
    for term in terms:
        term[...] = jnp.zeros(term.shape, term.dtype)


def backs_of(scal, step):
    near, far = step, 15 - step
    odd = scal[2] == 1
    return [jnp.where(odd, far, near), jnp.where(odd, near, far)]


class Near:
    def __init__(self, scal, a, b):
        self.even, self.a, self.b = scal[2] == 0, a, b

    def __getitem__(self, at):
        return jnp.where(self.even, self.a[at], self.b[at])


def pack_kernel(k_ref, v_ref, out_ref):
    out_ref[:, :WIDE] = k_ref[...]
    out_ref[:, WIDE:] = v_ref[...]


def own_forward_kernel(scal, first_ref, q_ref, g_ref, own, top, total, acc, e, gp, turned):
    top[...] = jnp.full(top.shape, neg_big, jnp.float32)
    total[...] = jnp.zeros(total.shape, jnp.float32)
    acc[...] = jnp.zeros(acc.shape, jnp.float32)
    forward_part(scal, first_ref, q_ref, g_ref, [own], [0], top, total, acc, e, gp)
    for g in range(KVH):
        turned[g] = heads_of(g_ref, g).astype(jnp.float32).T


def forward_kernel(kind, step, scal, first_ref, q_ref, g_ref, top_in, total_in, acc_in, *rest):
    blocks, (top, total, acc, e, gp) = rest[:-5], rest[-5:]
    top[...] = top_in[...]
    total[...] = total_in[...]
    acc[...] = acc_in[...]

    @pl.when(scal[1] >= step)
    def _():
        if kind == "near":
            a1, b1, a2, b2 = blocks
            use, backs = [Near(scal, a1, b1), Near(scal, a2, b2)], [1, 2]
        else:
            use, backs = list(blocks), backs_of(scal, step)[: len(blocks)]
        forward_part(scal, first_ref, q_ref, g_ref, use, backs, top, total, acc, e, gp)


def middle_kernel(
    scal, first_ref, q_ref, g_ref, turned, top_in, total_in, acc_in, e_a, gp_a, a, b,
    attended, log_ref, inner_ref, gq_acc, term_a, term_b, e_b, gp_b,
):
    log_ref[...] = top_in[...]
    inner_ref[...] = total_in[...]
    attended[...] = acc_in[...]
    gq_acc[...] = jnp.zeros(gq_acc.shape, jnp.float32)

    @pl.when(scal[1] >= STEPS)
    def _():
        backs = backs_of(scal, STEPS)[1:]
        forward_part(
            scal, first_ref, q_ref, g_ref, [b], backs, log_ref, inner_ref, attended, e_b, gp_b
        )

    inverse = []
    for g in range(KVH):
        total = inner_ref[g]
        inverse.append(1.0 / total)
        attended[g] = attended[g] * inverse[g]
        log_ref[g] = log_ref[g] + jnp.log2(total)
        inner_ref[g] = jnp.sum(attended[g] * turned[g], axis=0, keepdims=True)

    @pl.when(scal[1] >= STEPS)
    def _():
        backward_part(
            q_ref, g_ref, [a], factors_of(top_in, log_ref), inner_ref, gq_acc, e_a, gp_a, [term_a]
        )
        backward_part(q_ref, g_ref, [b], inverse, inner_ref, gq_acc, e_b, gp_b, [term_b])

    @pl.when(scal[1] < STEPS)
    def _():
        clear([term_a, term_b])


def pair_back(step, scal, q_ref, g_ref, log_ref, inner_ref, top, e, gp, a, b, acc, term_a, term_b):
    @pl.when(scal[1] >= step)
    def _():
        backward_part(
            q_ref, g_ref, [a, b], factors_of(top, log_ref), inner_ref, acc, e, gp, [term_a, term_b]
        )

    @pl.when(scal[1] < step)
    def _():
        clear([term_a, term_b])


def back_kernel(
    step, scal, q_ref, g_ref, log_ref, inner_ref, acc_in, top, e, gp, a, b, acc, term_a, term_b
):
    acc[...] = acc_in[...]
    pair_back(step, scal, q_ref, g_ref, log_ref, inner_ref, top, e, gp, a, b, acc, term_a, term_b)


def second_kernel(
    step, scal, q_ref, g_ref, log_ref, inner_ref, acc_in, top, e, gp, a, b, attended,
    acc, term_a, term_b, out_ref,
):
    acc[...] = acc_in[...]
    pair_back(step, scal, q_ref, g_ref, log_ref, inner_ref, top, e, gp, a, b, acc, term_a, term_b)
    for g in range(KVH):
        put_heads(out_ref, g, attended[g])


def near_back_kernel(
    scal, q_ref, g_ref, log_ref, inner_ref, acc_in, top, e, gp, a1, b1, a2, b2,
    acc, term_a1, term_b1, term_a2, term_b2,
):
    acc[...] = acc_in[...]
    clear([term_a1, term_b1, term_a2, term_b2])

    def run(blocks, terms):
        backward_part(
            q_ref, g_ref, blocks, factors_of(top, log_ref), inner_ref, acc, e, gp, terms
        )

    @pl.when((scal[1] >= 1) & (scal[2] == 0))
    def _():
        run([a1, a2], [term_a1, term_a2])

    @pl.when((scal[1] >= 1) & (scal[2] == 1))
    def _():
        run([b1, b2], [term_b1, term_b2])


def own_back_kernel(
    scal, q_ref, g_ref, log_ref, inner_ref, acc_in, top, e, gp, own, gq_ref, term_0, acc
):
    acc[...] = acc_in[...]
    backward_part(
        q_ref, g_ref, [own], factors_of(top, log_ref), inner_ref, acc, e, gp, [term_0]
    )
    for g in range(KVH):
        put_heads(gq_ref, g, acc[g] * SCALE)


ROW = jax.ShapeDtypeStruct((KVH, 1, LANES), jnp.float32)
TURNED = jax.ShapeDtypeStruct((KVH, HD, LANES), jnp.float32)


def call(kernel, outs, work, scal, *operands, scratch=()):
    in_vmem = pl.BlockSpec(memory_space=pltpu.VMEM)
    return pl.pallas_call(
        kernel,
        out_shape=outs,
        in_specs=[pl.BlockSpec(memory_space=pltpu.SMEM)] + [in_vmem] * len(operands),
        out_specs=[in_vmem] * len(outs),
        scratch_shapes=list(scratch),
        compiler_params=pltpu.CompilerParams(vmem_limit_bytes=24 * 1024 * 1024),
        cost_estimate=pl.CostEstimate(
            flops=int(work * 1.0e9), bytes_accessed=4 * 1024 * 1024, transcendentals=1 << 20
        ),
    )(scal, *operands)


def pack(keys, values):
    rows = keys.shape[0]
    return pl.pallas_call(
        pack_kernel,
        out_shape=jax.ShapeDtypeStruct((rows, 2 * WIDE), keys.dtype),
        in_specs=[pl.BlockSpec(memory_space=pltpu.VMEM)] * 2,
        out_specs=pl.BlockSpec(memory_space=pltpu.VMEM),
    )(keys, values)


def both_ways(x, near_pairs, far_pairs, flip):
    windows, count = lax.axis_size("dp"), lax.axis_size("ctx")
    pairs = []
    for window in range(windows):
        chosen = near_pairs if flip else far_pairs
        pairs += [(window * count + i, window * count + j) for i, j in chosen]
    return lax.ppermute(x, ("dp", "ctx"), pairs)


def gather_pairs(step, count):
    near = [(j, j + 1) for j in range(step - 1, count - 1)]
    blocks = range(count - STEPS - 1)
    start = 0 if step == 1 else step
    far = [((b - start) % count, (b - step - 1) % count) for b in blocks]
    return near, far


def return_pairs(step, count):
    near = [(j, j - 1) for j in range(STEPS + 1 - step, count)]
    blocks = range(count - STEPS - 1)
    end = STEPS + 1 + step if step < STEPS else count
    far = [((b + STEPS + step) % count, (b + end) % count) for b in blocks]
    return near, far


def add_low(a, b):
    return a + b


def local(queries, keys, values, out_grad, segment_ids):
    rows = queries.shape[0]
    count = lax.axis_size("ctx")
    odd = jnp.ones((), jnp.int32)
    q_start = lax.axis_index("ctx") * rows
    own = pack(keys, values)
    q_seg = lax.dynamic_slice_in_dim(segment_ids, q_start, rows, 0)
    first = jnp.sum((segment_ids[:, None] < q_seg[None, :]).astype(jnp.int32), axis=0, keepdims=True)
    scal = jnp.stack([q_start, (q_start - first[0, 0] + rows - 1) // rows, odd]).astype(jnp.int32)

    block = jax.ShapeDtypeStruct(own.shape, jnp.bfloat16)
    exact = jax.ShapeDtypeStruct(own.shape, jnp.float32)
    wide = jax.ShapeDtypeStruct(queries.shape, jnp.bfloat16)
    state = [ROW, ROW, TURNED]
    one = [jax.ShapeDtypeStruct((KVH, rows, LANES), jnp.bfloat16)] * 2
    two = [jax.ShapeDtypeStruct((KVH, 2 * rows, LANES), jnp.bfloat16)] * 2
    *now, e, gp, turned = call(
        own_forward_kernel, state + one + [TURNED], 1.0, scal, first, queries, out_grad, own
    )
    kept = {0: (now[0], e, gp)}

    def forward(kind, step, *blocks):
        *state_now, e, gp = call(
            functools.partial(forward_kernel, kind, step), state + (one if kind == "a" else two), 1.0,
            scal, first, queries, out_grad, *now, *blocks,
        )
        kept[step] = (state_now[0], e, gp)
        return state_now

    a, b, tops = [own], [own], {1: now[0]}
    for step in range(1, STEPS + 1):
        pairs = gather_pairs(step, count)
        to_a = a[-1]
        if step == 2 or step >= 4:
            to_a, _ = lax.optimization_barrier((to_a, tops[max(step - 2, 1)]))
        a.append(both_ways(to_a, *pairs, 0))
        b.append(both_ways(b[-1], *pairs, 1))
        if step == 2:
            now = forward("near", 1, a[1], b[1], a[2], b[2])
        elif 3 <= step < STEPS:
            now = forward("pair", step, a[step], b[step])
        tops[step] = now[0]
    now = forward("a", STEPS, a[STEPS])
    part = pltpu.VMEM(one[0].shape, jnp.bfloat16)
    attended_t, log_total, inner, acc, sum_a, sum_b = call(
        middle_kernel, [TURNED, ROW, ROW, TURNED, block, block], 1.5,
        scal, first, queries, out_grad, turned, *now, *kept[STEPS][1:], a[STEPS], b[STEPS],
        scratch=[part, part],
    )

    def backward(kernel, outs, step, *operands, scratch=()):
        return call(
            kernel, outs, 1.0, scal, queries, out_grad, log_total, inner, acc, *kept[step], *operands,
            scratch=scratch,
        )

    for step in range(1, STEPS + 1):
        pairs = return_pairs(step, count)
        sum_a = both_ways(sum_a, *pairs, 0)
        sum_b = both_ways(sum_b, *pairs, 1)
        back = STEPS - step
        if back == 6:
            acc, term_a, term_b, attended = backward(
                functools.partial(second_kernel, back), [TURNED, block, block, wide], back,
                a[back], b[back], attended_t,
            )
        elif back >= 3:
            acc, term_a, term_b = backward(
                functools.partial(back_kernel, back), [TURNED, block, block], back, a[back], b[back]
            )
        elif back == 2:
            acc, *terms = backward(
                near_back_kernel, [TURNED] + [block] * 4, 1, a[1], b[1], a[2], b[2]
            )
            term_a, term_b = terms[2:]
        elif back == 1:
            term_a, term_b = terms[:2]
            acc, _ = lax.optimization_barrier((acc, sum_a))
            grad_query, term_0 = backward(
                own_back_kernel, [wide, exact], 0, own, scratch=[pltpu.VMEM(TURNED.shape, jnp.float32)]
            )
        if back >= 1:
            sum_a, sum_b = add_low(sum_a, term_a), add_low(sum_b, term_b)
    summed = sum_a.astype(jnp.float32) + sum_b.astype(jnp.float32) + term_0
    return (attended, grad_query, summed[:, :WIDE], summed[:, WIDE:])


def solution(mesh):
    placed = P(("dp", "ctx"), None)
    return jax.shard_map(
        local,
        mesh=mesh,
        in_specs=(placed, placed, placed, placed, P("dp")),
        out_specs=(placed, placed, placed, placed),
        check_vma=False,
    )
```

```python
import functools
import math

import jax
import jax.numpy as jnp
from jax import lax
from jax.experimental import pallas as pl
from jax.experimental.pallas import tpu as pltpu
from jax.sharding import PartitionSpec as P

KVH = 4
HD = 128
GROUP = 4
WIDE = KVH * HD
FAR = 12
STEPS = 7
LANES = GROUP * 128
SCALE = 1.0 / math.sqrt(HD)
TO_TWO = SCALE / math.log(2.0)

neg_big = -1e30


def dot_nt(a, b):
    return lax.dot_general(a, b, (((1,), (1,)), ((), ())), preferred_element_type=jnp.float32)


def dot_nn(a, b):
    return lax.dot_general(a, b, (((1,), (0,)), ((), ())), preferred_element_type=jnp.float32)


def dot_tn(a, b):
    return lax.dot_general(a, b, (((0,), (0,)), ((), ())), preferred_element_type=jnp.float32)


def heads_of(ref, g):
    base = g * GROUP * HD
    return jnp.concatenate(
        [ref[:, base + r * HD : base + (r + 1) * HD] for r in range(GROUP)], axis=0
    )


def put_heads(ref, g, turned):
    flat = turned.T
    rows = ref.shape[0]
    for r in range(GROUP):
        cols = slice((g * GROUP + r) * HD, (g * GROUP + r + 1) * HD)
        ref[:, cols] = flat[r * rows : (r + 1) * rows].astype(ref.dtype)


def keys_of(blocks, g):
    return jnp.concatenate([b[:, g * HD : (g + 1) * HD] for b in blocks], axis=0)


def values_of(blocks, g):
    return jnp.concatenate([b[:, WIDE + g * HD : WIDE + (g + 1) * HD] for b in blocks], axis=0)


def allowed_keys(scal, first_ref, backs, rows):
    q_start = scal[0]
    first = jnp.concatenate([first_ref[...]] * GROUP, axis=1)
    within = lax.broadcasted_iota(jnp.int32, (rows, LANES), 0)
    parts = []
    for back in backs:
        place = (q_start - back * rows) + within
        seen = place >= first
        if isinstance(back, int) and back == 0:
            lanes = lax.broadcasted_iota(jnp.int32, (rows, LANES), 1)
            seen = seen & (within <= jnp.bitwise_and(lanes, rows - 1))
        parts.append(seen)
    return jnp.concatenate(parts, axis=0)


def forward_part(scal, first_ref, q_ref, g_ref, blocks, backs, top_ref, sum_ref, acc_ref, e_ref, gp_ref):
    allowed = allowed_keys(scal, first_ref, backs, q_ref.shape[0])
    for g in range(KVH):
        v = values_of(blocks, g)
        s = dot_nt(keys_of(blocks, g), heads_of(q_ref, g)) * TO_TWO
        s = jnp.where(allowed, s, neg_big)
        top = top_ref[g]
        new_top = jnp.maximum(top, jnp.max(s, axis=0, keepdims=True))
        e = jnp.exp2(s - new_top)
        shrink = jnp.exp2(top - new_top)
        e_low = e.astype(jnp.bfloat16)
        e_ref[g] = e_low
        gp_ref[g] = dot_nt(v, heads_of(g_ref, g)).astype(jnp.bfloat16)
        top_ref[g] = new_top
        sum_ref[g] = sum_ref[g] * shrink + jnp.sum(e, axis=0, keepdims=True)
        acc_ref[g] = acc_ref[g] * shrink + dot_tn(v, e_low)


def backward_part(q_ref, g_ref, blocks, factors, inner_ref, acc_ref, e_ref, gp_ref, outs):
    rows = q_ref.shape[0]
    for g in range(KVH):
        probs = e_ref[g].astype(jnp.float32) * factors[g]
        grad_scores = (probs * (gp_ref[g].astype(jnp.float32) - inner_ref[g])).astype(jnp.bfloat16)
        acc_ref[g] = acc_ref[g] + dot_tn(keys_of(blocks, g), grad_scores)
        grad_k = dot_nn(grad_scores, heads_of(q_ref, g)) * SCALE
        grad_v = dot_nn(probs.astype(jnp.bfloat16), heads_of(g_ref, g))
        for i, out in enumerate(outs):
            part = slice(i * rows, (i + 1) * rows)
            out[:, g * HD : (g + 1) * HD] = grad_k[part].astype(out.dtype)
            out[:, WIDE + g * HD : WIDE + (g + 1) * HD] = grad_v[part].astype(out.dtype)


def factors_of(top_ref, log_ref):
    return [jnp.exp2(top_ref[g] - log_ref[g]) for g in range(KVH)]


def clear(terms):
    for term in terms:
        term[...] = jnp.zeros(term.shape, term.dtype)


def backs_of(scal, step):
    near, far = step, 15 - step
    odd = scal[2] == 1
    return [jnp.where(odd, far, near), jnp.where(odd, near, far)]


class Near:
    def __init__(self, scal, a, b):
        self.even, self.a, self.b = scal[2] == 0, a, b

    def __getitem__(self, at):
        return jnp.where(self.even, self.a[at], self.b[at])


def pack_kernel(k_ref, v_ref, out_ref):
    out_ref[:, :WIDE] = k_ref[...]
    out_ref[:, WIDE:] = v_ref[...]


def own_forward_kernel(scal, first_ref, q_ref, g_ref, own, top, total, acc, e, gp, turned):
    top[...] = jnp.full(top.shape, neg_big, jnp.float32)
    total[...] = jnp.zeros(total.shape, jnp.float32)
    acc[...] = jnp.zeros(acc.shape, jnp.float32)
    forward_part(scal, first_ref, q_ref, g_ref, [own], [0], top, total, acc, e, gp)
    for g in range(KVH):
        turned[g] = heads_of(g_ref, g).astype(jnp.float32).T


def forward_kernel(kind, step, scal, first_ref, q_ref, g_ref, top_in, total_in, acc_in, *rest):
    blocks, (top, total, acc, e, gp) = rest[:-5], rest[-5:]
    top[...] = top_in[...]
    total[...] = total_in[...]
    acc[...] = acc_in[...]

    @pl.when(scal[1] >= step)
    def _():
        if kind == "near":
            a1, b1, a2, b2 = blocks
            use, backs = [Near(scal, a1, b1), Near(scal, a2, b2)], [1, 2]
        else:
            use, backs = list(blocks), backs_of(scal, step)[: len(blocks)]
        forward_part(scal, first_ref, q_ref, g_ref, use, backs, top, total, acc, e, gp)


def middle_kernel(
    scal, first_ref, q_ref, g_ref, turned, top_in, total_in, acc_in, e_a, gp_a, a, b,
    attended, log_ref, inner_ref, gq_acc, term_a, term_b, e_b, gp_b,
):
    log_ref[...] = top_in[...]
    inner_ref[...] = total_in[...]
    attended[...] = acc_in[...]
    gq_acc[...] = jnp.zeros(gq_acc.shape, jnp.float32)

    @pl.when(scal[1] >= STEPS)
    def _():
        backs = backs_of(scal, STEPS)[1:]
        forward_part(
            scal, first_ref, q_ref, g_ref, [b], backs, log_ref, inner_ref, attended, e_b, gp_b
        )

    inverse = []
    for g in range(KVH):
        total = inner_ref[g]
        inverse.append(1.0 / total)
        attended[g] = attended[g] * inverse[g]
        log_ref[g] = log_ref[g] + jnp.log2(total)
        inner_ref[g] = jnp.sum(attended[g] * turned[g], axis=0, keepdims=True)

    @pl.when(scal[1] >= STEPS)
    def _():
        backward_part(
            q_ref, g_ref, [a], factors_of(top_in, log_ref), inner_ref, gq_acc, e_a, gp_a, [term_a]
        )
        backward_part(q_ref, g_ref, [b], inverse, inner_ref, gq_acc, e_b, gp_b, [term_b])

    @pl.when(scal[1] < STEPS)
    def _():
        clear([term_a, term_b])


def pair_back(step, scal, q_ref, g_ref, log_ref, inner_ref, top, e, gp, a, b, acc, term_a, term_b):
    @pl.when(scal[1] >= step)
    def _():
        backward_part(
            q_ref, g_ref, [a, b], factors_of(top, log_ref), inner_ref, acc, e, gp, [term_a, term_b]
        )

    @pl.when(scal[1] < step)
    def _():
        clear([term_a, term_b])


def back_kernel(
    step, scal, q_ref, g_ref, log_ref, inner_ref, acc_in, top, e, gp, a, b, acc, term_a, term_b
):
    acc[...] = acc_in[...]
    pair_back(step, scal, q_ref, g_ref, log_ref, inner_ref, top, e, gp, a, b, acc, term_a, term_b)


def second_kernel(
    step, scal, q_ref, g_ref, log_ref, inner_ref, acc_in, top, e, gp, a, b, attended,
    acc, term_a, term_b, out_ref,
):
    acc[...] = acc_in[...]
    pair_back(step, scal, q_ref, g_ref, log_ref, inner_ref, top, e, gp, a, b, acc, term_a, term_b)
    for g in range(KVH):
        put_heads(out_ref, g, attended[g])


def near_back_kernel(
    scal, q_ref, g_ref, log_ref, inner_ref, acc_in, top, e, gp, a1, b1, a2, b2,
    acc, term_a1, term_b1, term_a2, term_b2,
):
    acc[...] = acc_in[...]
    clear([term_a1, term_b1, term_a2, term_b2])

    def run(blocks, terms):
        backward_part(
            q_ref, g_ref, blocks, factors_of(top, log_ref), inner_ref, acc, e, gp, terms
        )

    @pl.when((scal[1] >= 1) & (scal[2] == 0))
    def _():
        run([a1, a2], [term_a1, term_a2])

    @pl.when((scal[1] >= 1) & (scal[2] == 1))
    def _():
        run([b1, b2], [term_b1, term_b2])


def own_back_kernel(
    scal, q_ref, g_ref, log_ref, inner_ref, acc_in, top, e, gp, own, gq_ref, term_0, acc
):
    acc[...] = acc_in[...]
    backward_part(
        q_ref, g_ref, [own], factors_of(top, log_ref), inner_ref, acc, e, gp, [term_0]
    )
    for g in range(KVH):
        put_heads(gq_ref, g, acc[g] * SCALE)


ROW = jax.ShapeDtypeStruct((KVH, 1, LANES), jnp.float32)
TURNED = jax.ShapeDtypeStruct((KVH, HD, LANES), jnp.float32)


def call(kernel, outs, work, scal, *operands, scratch=()):
    in_vmem = pl.BlockSpec(memory_space=pltpu.VMEM)
    return pl.pallas_call(
        kernel,
        out_shape=outs,
        in_specs=[pl.BlockSpec(memory_space=pltpu.SMEM)] + [in_vmem] * len(operands),
        out_specs=[in_vmem] * len(outs),
        scratch_shapes=list(scratch),
        compiler_params=pltpu.CompilerParams(vmem_limit_bytes=24 * 1024 * 1024),
        cost_estimate=pl.CostEstimate(
            flops=int(work * 1.0e9), bytes_accessed=4 * 1024 * 1024, transcendentals=1 << 20
        ),
    )(scal, *operands)


def pack(keys, values):
    rows = keys.shape[0]
    return pl.pallas_call(
        pack_kernel,
        out_shape=jax.ShapeDtypeStruct((rows, 2 * WIDE), keys.dtype),
        in_specs=[pl.BlockSpec(memory_space=pltpu.VMEM)] * 2,
        out_specs=pl.BlockSpec(memory_space=pltpu.VMEM),
    )(keys, values)


def both_ways(x, near_pairs, far_pairs, flip):
    windows, count = lax.axis_size("dp"), lax.axis_size("ctx")
    pairs = []
    for window in range(windows):
        chosen = near_pairs if flip else far_pairs
        pairs += [(window * count + i, window * count + j) for i, j in chosen]
    return lax.ppermute(x, ("dp", "ctx"), pairs)


def gather_pairs(step, count):
    near = [(j, j + 1) for j in range(step - 1, count - 1)]
    blocks = range(count - STEPS - 1)
    start = 0 if step == 1 else step
    far = [((b - start) % count, (b - step - 1) % count) for b in blocks]
    return near, far


def return_pairs(step, count):
    near = [(j, j - 1) for j in range(STEPS + 1 - step, count)]
    if step <= FAR - STEPS - 1:
        far = [(z, z + 1) for z in range(STEPS + step, count - 1)]
        far.append((count - 1, count - 1 - STEPS - step))
    else:
        begin, end = {5: (0, 2), 6: (2, 3), 7: (3, 4)}[step]
        far = [((b + FAR + begin) % count, (b + FAR + end) % count) for b in range(count - FAR)]
    return near, far


def add_low(a, b):
    return a + b


def local(queries, keys, values, out_grad, segment_ids):
    rows = queries.shape[0]
    count = lax.axis_size("ctx")
    odd = jnp.ones((), jnp.int32)
    q_start = lax.axis_index("ctx") * rows
    own = pack(keys, values)
    q_seg = lax.dynamic_slice_in_dim(segment_ids, q_start, rows, 0)
    first = jnp.sum((segment_ids[:, None] < q_seg[None, :]).astype(jnp.int32), axis=0, keepdims=True)
    scal = jnp.stack([q_start, (q_start - first[0, 0] + rows - 1) // rows, odd]).astype(jnp.int32)

    block = jax.ShapeDtypeStruct(own.shape, jnp.bfloat16)
    exact = jax.ShapeDtypeStruct(own.shape, jnp.float32)
    wide = jax.ShapeDtypeStruct(queries.shape, jnp.bfloat16)
    state = [ROW, ROW, TURNED]
    one = [jax.ShapeDtypeStruct((KVH, rows, LANES), jnp.bfloat16)] * 2
    two = [jax.ShapeDtypeStruct((KVH, 2 * rows, LANES), jnp.bfloat16)] * 2
    *now, e, gp, turned = call(
        own_forward_kernel, state + one + [TURNED], 1.0, scal, first, queries, out_grad, own
    )
    kept = {0: (now[0], e, gp)}

    def forward(kind, step, *blocks):
        *state_now, e, gp = call(
            functools.partial(forward_kernel, kind, step), state + (one if kind == "a" else two), 1.0,
            scal, first, queries, out_grad, *now, *blocks,
        )
        kept[step] = (state_now[0], e, gp)
        return state_now

    a, b, tops = [own], [own], {1: now[0]}
    for step in range(1, STEPS + 1):
        pairs = gather_pairs(step, count)
        to_a = a[-1]
        if step == 2 or step >= 4:
            to_a, _ = lax.optimization_barrier((to_a, tops[max(step - 2, 1)]))
        a.append(both_ways(to_a, *pairs, 0))
        b.append(both_ways(b[-1], *pairs, 1))
        if step == 2:
            now = forward("near", 1, a[1], b[1], a[2], b[2])
        elif 3 <= step < STEPS:
            now = forward("pair", step, a[step], b[step])
        tops[step] = now[0]
    now = forward("a", STEPS, a[STEPS])
    part = pltpu.VMEM(one[0].shape, jnp.bfloat16)
    attended_t, log_total, inner, acc, sum_a, sum_b = call(
        middle_kernel, [TURNED, ROW, ROW, TURNED, block, block], 1.5,
        scal, first, queries, out_grad, turned, *now, *kept[STEPS][1:], a[STEPS], b[STEPS],
        scratch=[part, part],
    )

    def backward(kernel, outs, step, *operands, scratch=()):
        return call(
            kernel, outs, 1.0, scal, queries, out_grad, log_total, inner, acc, *kept[step], *operands,
            scratch=scratch,
        )

    early = []
    for step in range(1, STEPS + 1):
        pairs = return_pairs(step, count)
        sum_a = both_ways(sum_a, *pairs, 0)
        sum_b = both_ways(sum_b, *pairs, 1)
        back = STEPS - step
        if back >= 3:
            early.append(sum_a.astype(jnp.float32))
        if back == 6:
            acc, term_a, term_b, attended = backward(
                functools.partial(second_kernel, back), [TURNED, block, block, wide], back,
                a[back], b[back], attended_t,
            )
        elif back >= 3:
            acc, term_a, term_b = backward(
                functools.partial(back_kernel, back), [TURNED, block, block], back, a[back], b[back]
            )
        elif back == 2:
            acc, *terms = backward(
                near_back_kernel, [TURNED] + [block] * 4, 1, a[1], b[1], a[2], b[2]
            )
            term_a, term_b = terms[2:]
        elif back == 1:
            term_a, term_b = terms[:2]
            acc, _ = lax.optimization_barrier((acc, sum_a))
            grad_query, term_0 = backward(
                own_back_kernel, [wide, exact], 0, own, scratch=[pltpu.VMEM(TURNED.shape, jnp.float32)]
            )
        if back >= 1:
            sum_a, sum_b = add_low(sum_a, term_a), add_low(sum_b, term_b)
    summed = sum_a.astype(jnp.float32) + sum_b.astype(jnp.float32) + term_0
    summed = summed + jnp.where(q_start <= STEPS * rows, sum(early), 0.0)
    return (attended, grad_query, summed[:, :WIDE], summed[:, WIDE:])


def solution(mesh):
    placed = P(("dp", "ctx"), None)
    return jax.shard_map(
        local,
        mesh=mesh,
        in_specs=(placed, placed, placed, placed, P("dp")),
        out_specs=(placed, placed, placed, placed),
        check_vma=False,
    )
```
